128 devices in a mesh: dp: 32 (over y, x, core), tensor: 4 (over z).
Axes of the slice: x: 4, y: 4, z: 4, core: 2. Of those that a mesh axis runs over, the one named last changes fastest.
Arguments:
- tokens: bfloat16 [77824, 768], P(('dp', 'tensor')), may hold values from -6 to 6
- prompt_table: float32 [100, 768], replicated, may hold values from -6 to 6
- lengths: int32 [256], P('dp'), may hold values from 1 to 100, as said below
- table_rows: int32 [256, 100], P('dp'), may hold values from 0 to 99
- ln1_gain: float32 [768], replicated, may hold values from 0.1 to 1.9
- ln1_bias: float32 [768], replicated, may hold values from -3 to 3
- w_qkv: float32 [3, 768, 768], P(None, 'dp', 'tensor'), may hold values from -0.21875 to 0.21875
- qv_bias: float32 [2, 768], P(None, 'tensor'), may hold values from -1.5 to 1.5
- w_out: float32 [768, 768], P('tensor', 'dp'), may hold values from -0.875 to 0.875
- out_bias: float32 [768], replicated, may hold values from -3 to 3
- ln2_gain: float32 [768], replicated, may hold values from 0.1 to 1.9
- ln2_bias: float32 [768], replicated, may hold values from -3 to 3
- w_up: float32 [768, 3072], P('dp', 'tensor'), may hold values from -0.21875 to 0.21875
- up_bias: float32 [3072], P('tensor'), may hold values from -3 to 3
- w_down: float32 [3072, 768], P('tensor', 'dp'), may hold values from -0.109375 to 0.109375
- down_bias: float32 [768], replicated, may hold values from -3 to 3
- cotangent: bfloat16 [77824, 768], P(('dp', 'tensor')), may hold values from -6 to 6
Outputs:
- output: bfloat16 [77824, 768], P(('dp', 'tensor'))
- token_grad: float32 [77824, 768], P(('dp', 'tensor'))
- table_grad: float32 [100, 768], replicated
The draws below stay inside these ranges and needn't reach their ends.
Inputs may be any that keep to these rules, and one draw needn't show every extreme that they name: `lengths`: each image's prompt length is one of 1, 10, 50 and 100; in every draw some image has 100 and some has 1. `table_rows`: only the first lengths[i] slots of image i are used.
All inputs are finite; a program needn't handle non-finite values.
Results may differ from the reference program's by a relative error of at most 0.012.
The reference program's roundings to bfloat16 on the way count: a program that leaves them out, or rounds other values in their place, can miss the bound.
Values may be sent and summed in bfloat16 or wider, within the bound.
A program may use at most 128 MiB of HBM per device.

```python
import jax
import jax.numpy as jnp
from jax import lax

D = 768
HEADS = 12
HD = 64
FF = 3072
PATCHES = 197
PROMPTS = 100
IMG_DEV = 8
SEQ = 304
IMAGES = 256
TOKENS = 77824


def draw_lengths(key, part):
    key = jax.random.fold_in(key, 11)
    split_keys = jax.random.split(key, 2)
    options = jnp.array([1, max(1, PROMPTS // 10), PROMPTS // 2, PROMPTS], dtype=jnp.int32)
    chosen = jax.random.randint(split_keys[0], (IMAGES,), 0, 4)
    lengths_out = jnp.take(options, chosen)
    leader = jax.random.randint(split_keys[1], (), 0, IMAGES)
    places = jnp.arange(IMAGES, dtype=jnp.int32)
    lengths_out = jnp.where(places == leader, PROMPTS, lengths_out)
    lengths_out = jnp.where(places == (leader + 1) % IMAGES, 1, lengths_out)
    return lengths_out.astype(jnp.int32)


def with_ends(entries, own_key, least, high):
    shape = entries.shape
    index_at = [jax.random.randint(jax.random.fold_in(own_key, axis), (), 0, shape[axis]) for axis in range(len(shape))]
    entries = entries.at[tuple(index_at)].set(least)
    longest = shape.index(max(shape))
    index_at[longest] = (index_at[longest] + 1) % shape[longest]
    return entries.at[tuple(index_at)].set(high)


def steps_of(stream_key, dims, shards, least, largest):
    loudness, own = 1.0, jax.random.fold_in(stream_key, 6)
    for dim, blocks in shards:
        draws = jnp.exp(jax.random.uniform(jax.random.fold_in(own, dim), (blocks,), jnp.float32, least / len(shards), largest / len(shards)))
        loudness = loudness * jnp.repeat(draws, dims[dim] // blocks).reshape([-1 if axis == dim else 1 for axis in range(len(dims))])
    return loudness


def normal_values(stream_key, shape, width, bound, cuts=(), held_as=jnp.bfloat16):
    entries = jax.random.normal(stream_key, shape, jnp.float32) * width
    if len(cuts) > 0:
        entries = steps_of(stream_key, shape, cuts, -0.22, 0.18) * entries
    return jnp.clip(entries, min=-bound, max=bound).astype(held_as)


def setup_inputs(seed: int = 0) -> dict:
    seeds = jax.random.split(jax.random.key(seed), 18)
    tokens = normal_values(seeds[0], (TOKENS, D), 1.0, 6.0, ((0, 128),))
    prompt_table = normal_values(seeds[1], (PROMPTS, D), 1.0, 6.0, (), jnp.float32)
    lengths = draw_lengths(jax.random.fold_in(seeds[17], 71), 0)
    table_rows = with_ends(jax.random.randint(seeds[3], (IMAGES, PROMPTS), 0, PROMPTS), jax.random.fold_in(seeds[3], 1), 0, PROMPTS - 1).astype(jnp.int32)
    ln1_gain = jnp.clip(1.0 + 0.18 * jax.random.normal(seeds[4], (D,), jnp.float32), 0.1, 1.9)
    ln1_bias = normal_values(seeds[5], (D,), 0.5, 3.0, (), jnp.float32)
    w_qkv = normal_values(seeds[6], (3, D, D), D ** -0.5, 0.21875, ((1, 32), (2, 4)), jnp.float32)
    qv_bias = normal_values(seeds[7], (2, D), 0.25, 1.5, ((1, 4),), jnp.float32)
    w_out = normal_values(seeds[8], (D, D), (max(1, D // 16)) ** -0.5, 0.875, ((0, 4), (1, 32)), jnp.float32)
    out_bias = normal_values(seeds[9], (D,), 0.5, 3.0, (), jnp.float32)
    ln2_gain = jnp.clip(1.0 + 0.18 * jax.random.normal(seeds[10], (D,), jnp.float32), 0.1, 1.9)
    ln2_bias = normal_values(seeds[11], (D,), 0.5, 3.0, (), jnp.float32)
    w_up = normal_values(seeds[12], (D, FF), D ** -0.5, 0.21875, ((0, 32), (1, 4)), jnp.float32)
    up_bias = normal_values(seeds[13], (FF,), 0.5, 3.0, ((0, 4),), jnp.float32)
    w_down = normal_values(seeds[14], (FF, D), FF ** -0.5, 0.109375, ((0, 4), (1, 32)), jnp.float32)
    down_bias = normal_values(seeds[15], (D,), 0.5, 3.0, (), jnp.float32)
    cotangent = normal_values(seeds[16], (TOKENS, D), 1.0, 6.0, ((0, 128),))
    return dict(tokens=tokens, prompt_table=prompt_table, lengths=lengths, table_rows=table_rows, ln1_gain=ln1_gain, ln1_bias=ln1_bias, w_qkv=w_qkv, qv_bias=qv_bias, w_out=w_out, out_bias=out_bias, ln2_gain=ln2_gain, ln2_bias=ln2_bias, w_up=w_up, up_bias=up_bias, w_down=w_down, down_bias=down_bias, cotangent=cotangent)


@jax.custom_vjp
def low(v):
    return lax.optimization_barrier(v.astype(jnp.bfloat16)).astype(jnp.float32)

@jax.custom_vjp
def low_back(v):
    return v

def low_keep(v):
    return (low(v), None)

def low_pass(kept, grad):
    return (grad,)

def back_keep(v):
    return (v, None)

def back_low(kept, grad):
    return (low(grad),)
low.defvjp(low_keep, low_pass)
low_back.defvjp(back_keep, back_low)
EPSILON = 1e-06
MASKED_SCORE = -1e+30
HIGHEST = lax.Precision.HIGHEST

def layer_norm(hidden_in, norm_gain, norm_shift):
    average = lax.optimization_barrier(jnp.mean(hidden_in, axis=-1, keepdims=True))
    centered = hidden_in - average
    variance = lax.optimization_barrier(jnp.mean(centered * centered, axis=-1, keepdims=True))
    return centered * lax.rsqrt(variance + EPSILON) * norm_gain + norm_shift

def group_forward(prompt_table, weights, token_rows, lengths, table_rows):
    gain_one, shift_one, w_qkv, qv_bias, w_out, out_bias, gain_two, shift_two, w_up, up_bias, w_down, down_bias = weights
    image_count = lengths.shape[0]
    slot_ids = jnp.arange(SEQ, dtype=jnp.int32)
    key_live = slot_ids[None, :] < PATCHES + lengths[:, None]
    live_slot = (slot_ids[None, :] >= PATCHES) & key_live
    table_slot = jnp.clip(slot_ids - PATCHES, 0, PROMPTS - 1).astype(jnp.int32)
    picked = jnp.take(table_rows, table_slot, axis=1)
    prompt_rows = prompt_table[picked]
    inputs = jnp.where(live_slot[:, :, None], prompt_rows, token_rows.reshape(image_count, SEQ, D))
    inputs = inputs.reshape(image_count * SEQ, D)
    first_in = low(layer_norm(inputs, gain_one, shift_one))
    projected = jnp.einsum('rd,cdk->rck', first_in, w_qkv, precision=HIGHEST)
    queries = low(low_back(projected[:, 0] + qv_bias[0])).reshape(image_count, SEQ, HEADS, HD)
    key_rows = low(low_back(projected[:, 1])).reshape(image_count, SEQ, HEADS, HD)
    value_rows = low(low_back(projected[:, 2] + qv_bias[1])).reshape(image_count, SEQ, HEADS, HD)
    scores = jnp.einsum('iqhd,ikhd->ihqk', queries, key_rows, precision=HIGHEST) * HD ** (-0.5)
    scores = low_back(scores)
    scores = jnp.where(key_live[:, None, None, :], scores, MASKED_SCORE)
    probs_low = low(jax.nn.softmax(scores, axis=-1))
    attended = jnp.einsum('ihqk,ikhd->iqhd', probs_low, value_rows, precision=HIGHEST)
    attended = low(low_back(attended.reshape(image_count * SEQ, D)))
    middle = inputs + low_back(jnp.dot(attended, w_out, precision=HIGHEST) + out_bias)
    second_in = low(layer_norm(middle, gain_two, shift_two))
    upper = low_back(jnp.dot(second_in, w_up, precision=HIGHEST) + up_bias)
    hidden = low(jax.nn.gelu(upper, approximate=False))
    return middle + jnp.dot(hidden, w_down, precision=HIGHEST) + down_bias

def reference(tokens, prompt_table, lengths, table_rows, ln1_gain, ln1_bias, w_qkv, qv_bias, w_out, out_bias, ln2_gain, ln2_bias, w_up, up_bias, w_down, down_bias, cotangent):
    weights = (ln1_gain, ln1_bias, low(w_qkv), qv_bias, low(w_out), out_bias, ln2_gain, ln2_bias, low(w_up), up_bias, low(w_down), down_bias)
    blocks = lengths.shape[0] // IMG_DEV
    items = (lengths.reshape(blocks, IMG_DEV), table_rows.reshape(blocks, IMG_DEV, PROMPTS))

    def forward(token_all, table_all):

        def block_fn(rows_in, lens_in, picks_in):
            return group_forward(table_all, weights, rows_in, lens_in, picks_in)
        checked = jax.checkpoint(block_fn)

        def block_apply(block_item):
            return checked(block_item[0], block_item[1], block_item[2])
        stacked = (token_all.reshape(blocks, IMG_DEV * SEQ, D), items[0], items[1])
        outputs = lax.map(block_apply, stacked)
        return outputs.reshape(blocks * IMG_DEV * SEQ, D)
    result, pullback = jax.vjp(forward, tokens.astype(jnp.float32), prompt_table)
    token_grad, table_grad = pullback(cotangent.astype(jnp.float32))
    return (result.astype(jnp.bfloat16), token_grad, table_grad)
```

```python
import functools
import jax
import jax.numpy as jnp
from jax import lax
from jax.experimental import pallas as pl
from jax.experimental.pallas import tpu as pltpu
from jax.sharding import PartitionSpec as P

D = 768
HD = 64
PATCHES = 197
PROMPTS = 100
SEQ = 304
NZ = 4
HZ = 3
QW = 192
FZ = 768
EPSILON = 1e-06
MASKED = -1e30
F32 = jnp.float32
BF = jnp.bfloat16
NN = (((1,), (0,)), ((), ()))
NT = (((1,), (1,)), ((), ()))
TN = (((0,), (0,)), ((), ()))
CH = 32


def mm(a, b, dims=NN):
    return lax.dot_general(a, b, dims, preferred_element_type=F32)


def gelu_pair(u):
    a = jnp.abs(u)
    t = 1.0 / (1.0 + (0.3275911 * 0.7071067811865476) * a)
    e = jnp.exp(-0.5 * (u * u))
    poly = t * (0.254829592 + t * (-0.284496736 + t * (1.421413741 + t * (-1.453152027 + t * 1.061405429))))
    half = 0.5 * poly * e
    cdf = jnp.where(u >= 0, 1.0 - half, half)
    return u * cdf, cdf + u * (0.3989422804014327 * e)


def stats(h):
    mean = jnp.mean(h, axis=-1, keepdims=True)
    c = h - mean
    r = lax.rsqrt(jnp.mean(c * c, axis=-1, keepdims=True) + EPSILON)
    return c * r, r


def norm_back(g, n, r, gain):
    e = g * gain
    return r * (e - jnp.mean(e, axis=-1, keepdims=True) - n * jnp.mean(e * n, axis=-1, keepdims=True))


def compute(rows, lens, tok, table, trows, g1, b1, qvb, ob, g2, b2, upb, db, cot,
            wqkv, wout, wup, wdn, out, tgrad, pgrad,
            inp, fin, qkv, probs, att, mid, sin, hid, dup, dmid, dml, dat, dqkv):
    t = lax.axis_index("tensor")
    images = rows // SEQ
    hots = []
    for i in range(images):
        base = jnp.concatenate([trows[pl.ds(t * images + i, 1), :], jnp.full((1, 384 - PROMPTS), -1, jnp.int32)], axis=1)
        slot = pltpu.roll(base, PATCHES, 1)
        slot = slot[:, :SEQ]
        place = lax.broadcasted_iota(jnp.int32, (1, SEQ), 1)
        live = (place >= PATCHES) & (place < PATCHES + lens[t * images + i])
        slot = jnp.where(live, slot, -1)
        prow = lax.broadcasted_iota(jnp.int32, (PROMPTS, SEQ), 0)
        hots.append((prow == slot).astype(F32))
    for i in range(images):
        place = lax.broadcasted_iota(jnp.int32, (SEQ, 1), 0)
        live = (place >= PATCHES) & (place < PATCHES + lens[t * images + i])
        picked = lax.dot_general(hots[i], table[...], TN, precision=lax.Precision.HIGHEST, preferred_element_type=F32)
        inp[pl.ds(i * SEQ, SEQ), :] = jnp.where(live, picked, tok[pl.ds(i * SEQ, SEQ), :].astype(F32))

    @pl.loop(0, rows // CH)
    def _(c):
        sl = pl.ds(pl.multiple_of(c * CH, CH), CH)
        n, _ = stats(inp[sl, :])
        fin[sl, :] = (n * g1[...] + b1[...]).astype(BF)

    @pl.loop(0, NZ)
    def _(z):
        x = mm(fin[...], wqkv[z])
        qkv[z] = (x + qvb[z]).astype(BF)

    @pl.loop(0, NZ)
    def _(z):
        for i in range(images):
            rs = pl.ds(i * SEQ, SEQ)
            blk = qkv[z, rs, :]
            place = lax.broadcasted_iota(jnp.int32, (1, SEQ), 1)
            bias = jnp.where(place < PATCHES + lens[t * images + i], 0.0, MASKED)
            outs = []
            for h in range(HZ):
                q = blk[:, h * HD:(h + 1) * HD] * 0.125
                k = blk[:, QW + h * HD:QW + (h + 1) * HD]
                v = blk[:, 2 * QW + h * HD:2 * QW + (h + 1) * HD]
                s = mm(q.astype(BF), k, NT) + bias
                m = jnp.max(s, axis=-1, keepdims=True)
                e = jnp.exp(s - m)
                p = (e / jnp.sum(e, axis=-1, keepdims=True)).astype(BF)
                probs[z, i * HZ + h] = p
                outs.append(mm(p, v).astype(BF))
            att[z, rs, :] = jnp.concatenate(outs, axis=1)

    @pl.loop(0, images)
    def _(i):
        rs = pl.ds(pl.multiple_of(i * SEQ, SEQ), SEQ)
        acc = mm(att[0, rs, :], wout[0], NT)
        for z in range(1, NZ):
            acc += mm(att[z, rs, :], wout[z], NT)
        mid[rs, :] = inp[rs, :] + acc + ob[...]

    @pl.loop(0, rows // CH)
    def _(c):
        sl = pl.ds(pl.multiple_of(c * CH, CH), CH)
        n, _ = stats(mid[sl, :])
        sin[sl, :] = (n * g2[...] + b2[...]).astype(BF)

    TF = 256
    NF = FZ // TF

    @pl.loop(0, NZ * NF)
    def _(j):
        z = j // NF
        f = pl.ds(pl.multiple_of((j % NF) * TF, TF), TF)
        fo = pl.ds(pl.multiple_of(j * TF, TF), TF)
        for i in range(images):
            rs = pl.ds(i * SEQ, SEQ)
            u = mm(sin[rs, :], wup[z, :, f]) + upb[z, :, f]
            dh = mm(cot[rs, :], wdn[z, :, f])
            a, b = gelu_pair(u)
            hid[rs, fo] = a.astype(BF)
            dup[rs, fo] = (dh * b).astype(BF)

    @pl.loop(0, images)
    def _(i):
        rs = pl.ds(pl.multiple_of(i * SEQ, SEQ), SEQ)
        acc = mm(hid[rs, 0:FZ], wdn[0], NT)
        for z in range(1, NZ):
            acc += mm(hid[rs, z * FZ:(z + 1) * FZ], wdn[z], NT)
        out[rs, :] = (mid[rs, :] + acc + db[...]).astype(BF)

    @pl.loop(0, images)
    def _(i):
        rs = pl.ds(pl.multiple_of(i * SEQ, SEQ), SEQ)
        acc = mm(dup[rs, 0:FZ], wup[0], NT)
        for z in range(1, NZ):
            acc += mm(dup[rs, z * FZ:(z + 1) * FZ], wup[z], NT)
        dmid[rs, :] = acc

    @pl.loop(0, rows // CH)
    def _(c):
        sl = pl.ds(pl.multiple_of(c * CH, CH), CH)
        n, r = stats(mid[sl, :])
        d = cot[sl, :].astype(F32) + norm_back(dmid[sl, :], n, r, g2[...])
        dmid[sl, :] = d
        dml[sl, :] = d.astype(BF)

    @pl.loop(0, NZ)
    def _(z):
        dat[z] = mm(dml[...], wout[z]).astype(BF)

    @pl.loop(0, NZ)
    def _(z):
        for i in range(images):
            rs = pl.ds(i * SEQ, SEQ)
            blk = qkv[z, rs, :]
            db_ = dat[z, rs, :]
            dq, dk, dv = [], [], []
            for h in range(HZ):
                q = blk[:, h * HD:(h + 1) * HD]
                k = blk[:, QW + h * HD:QW + (h + 1) * HD]
                v = blk[:, 2 * QW + h * HD:2 * QW + (h + 1) * HD]
                do = db_[:, h * HD:(h + 1) * HD]
                p = probs[z, i * HZ + h]
                dp = mm(do, v, NT)
                dv.append(mm(p, do, TN).astype(BF))
                pf = p.astype(F32)
                x = dp * pf
                ds = (x - pf * jnp.sum(x, axis=-1, keepdims=True)).astype(BF)
                dq.append((mm(ds, k) * 0.125).astype(BF))
                dk.append((mm(ds, q, TN) * 0.125).astype(BF))
            dqkv[z, rs, :] = jnp.concatenate(dq + dk + dv, axis=1)

    @pl.loop(0, images)
    def _(i):
        rs = pl.ds(pl.multiple_of(i * SEQ, SEQ), SEQ)
        acc = mm(dqkv[0, rs, :], wqkv[0], NT)
        for z in range(1, NZ):
            acc += mm(dqkv[z, rs, :], wqkv[z], NT)
        tgrad[rs, :] = acc

    @pl.loop(0, rows // CH)
    def _(c):
        sl = pl.ds(pl.multiple_of(c * CH, CH), CH)
        n, r = stats(inp[sl, :])
        d = dmid[sl, :] + norm_back(tgrad[sl, :], n, r, g1[...])
        tgrad[sl, :] = d

    total = None
    for i in range(images):
        rs = pl.ds(i * SEQ, SEQ)
        place = lax.broadcasted_iota(jnp.int32, (SEQ, 1), 0)
        live = (place >= PATCHES) & (place < PATCHES + lens[t * images + i])
        d = tgrad[rs, :]
        part = lax.dot_general(hots[i], d, NN, precision=lax.Precision.HIGHEST, preferred_element_type=F32)
        total = part if total is None else total + part
        tgrad[rs, :] = jnp.where(live, 0.0, d)
    pgrad[...] = total


def local_call(tok, table, lens, trows, g1, b1, qvb, ob, g2, b2, upb, db, cot, wqkv, wout, wup, wdn):
    rows = tok.shape[0]
    V = pl.BlockSpec(memory_space=pltpu.VMEM)
    S = pl.BlockSpec(memory_space=pltpu.SMEM)
    images = rows // SEQ
    return pl.pallas_call(
        functools.partial(compute, rows),
        out_shape=(jax.ShapeDtypeStruct((rows, D), BF), jax.ShapeDtypeStruct((rows, D), F32), jax.ShapeDtypeStruct((PROMPTS, D), F32)),
        in_specs=[S] + [V] * 16,
        out_specs=(V, V, V),
        scratch_shapes=[
            pltpu.VMEM((rows, D), F32),
            pltpu.VMEM((rows, D), BF),
            pltpu.VMEM((NZ, rows, 3 * QW), BF),
            pltpu.VMEM((NZ, images * HZ, SEQ, SEQ), BF),
            pltpu.VMEM((NZ, rows, QW), BF),
            pltpu.VMEM((rows, D), F32),
            pltpu.VMEM((rows, D), BF),
            pltpu.VMEM((rows, NZ * FZ), BF),
            pltpu.VMEM((rows, NZ * FZ), BF),
            pltpu.VMEM((rows, D), F32),
            pltpu.VMEM((rows, D), BF),
            pltpu.VMEM((NZ, rows, QW), BF),
            pltpu.VMEM((NZ, rows, 3 * QW), BF),
        ],
        compiler_params=pltpu.CompilerParams(vmem_limit_bytes=60 * 2**20),
    )(lens, tok, table, trows, g1, b1, qvb, ob, g2, b2, upb, db, cot, wqkv, wout, wup, wdn)


def body(tokens, prompt_table, lengths, table_rows, ln1_gain, ln1_bias, w_qkv, qv_bias, w_out, out_bias,
         ln2_gain, ln2_bias, w_up, up_bias, w_down, down_bias, cotangent):
    blk = jnp.concatenate([w_qkv[0], w_qkv[1], w_qkv[2], w_out.T, w_up, w_down.T], axis=1).astype(BF)
    g = lax.all_gather(blk, "dp", axis=0, tiled=True)
    g = lax.all_gather(g, "tensor", axis=0)
    wqkv, wout, wup, wdn = g[:, :, :576], g[:, :, 576:768], g[:, :, 768:1536], g[:, :, 1536:]
    bias = jnp.concatenate([qv_bias[0], jnp.zeros_like(qv_bias[0]), qv_bias[1], up_bias])
    bg = lax.all_gather(bias, "tensor", axis=0)
    qvb = bg[:, None, :576]
    upb = bg[:, None, 576:]
    o, tg, pg = local_call(tokens, prompt_table, lengths, table_rows, ln1_gain[None], ln1_bias[None], qvb, out_bias[None],
                           ln2_gain[None], ln2_bias[None], upb, down_bias[None], cotangent, wqkv, wout, wup, wdn)
    return o, tg, lax.psum(pg, ("dp", "tensor"))


def solution(mesh):
    row = P(("dp", "tensor"), None)
    return jax.shard_map(
        body, mesh=mesh,
        in_specs=(row, P(), P("dp"), P("dp", None), P(), P(), P(None, "dp", "tensor"), P(None, "tensor"), P("tensor", "dp"),
                  P(), P(), P(), P("dp", "tensor"), P("tensor"), P("tensor", "dp"), P(), row),
        out_specs=(row, row, P()), check_vma=False)
```

```python
import functools
import jax
import jax.numpy as jnp
from jax import lax
from jax.experimental import pallas as pl
from jax.experimental.pallas import tpu as pltpu
from jax.sharding import PartitionSpec as P

D = 768
HD = 64
PATCHES = 197
PROMPTS = 100
SEQ = 304
NZ = 4
HZ = 3
QW = 192
FZ = 768
EPSILON = 1e-06
MASKED = -1e30
F32 = jnp.float32
BF = jnp.bfloat16
NN = (((1,), (0,)), ((), ()))
NT = (((1,), (1,)), ((), ()))
TN = (((0,), (0,)), ((), ()))
CH = 32
MESH = pl.DeviceIdType.MESH
ORDERS = ((0, 1, 2), (1, 2, 0), (2, 0, 1))


def mm(a, b, dims=NN):
    return lax.dot_general(a, b, dims, preferred_element_type=F32)


def gelu_pair(u):
    a = jnp.abs(u)
    t = 1.0 / (1.0 + (0.3275911 * 0.7071067811865476) * a)
    e = jnp.exp(-0.5 * (u * u))
    poly = t * (0.254829592 + t * (-0.284496736 + t * (1.421413741 + t * (-1.453152027 + t * 1.061405429))))
    half = 0.5 * poly * e
    cdf = jnp.where(u >= 0, 1.0 - half, half)
    return u * cdf, cdf + u * (0.3989422804014327 * e)


def stats(h):
    mean = jnp.mean(h, axis=-1, keepdims=True)
    c = h - mean
    r = lax.rsqrt(jnp.mean(c * c, axis=-1, keepdims=True) + EPSILON)
    return c * r, r


def norm_back(g, n, r, gain):
    e = g * gain
    return r * (e - jnp.mean(e, axis=-1, keepdims=True) - n * jnp.mean(e * n, axis=-1, keepdims=True))


class Gather:
    def __init__(self, G, stage, other, psem, ssem, rsem, fsem, gsem):
        dp = lax.axis_index("dp")
        z = lax.axis_index("tensor")
        self.core = lax.rem(dp, 2)
        chip = lax.div(dp, 2)
        self.at = (lax.rem(chip, 4), lax.div(chip, 4), z)
        self.G, self.stage, self.other = G, stage, other
        self.psem, self.ssem, self.rsem, self.fsem, self.gsem = psem, ssem, rsem, fsem, gsem

    def device(self, at, core):
        return ((at[1] * 4 + at[0]) * 2 + core, at[2])

    def moved(self, axis, step):
        at = list(self.at)
        at[axis] = lax.rem(at[axis] + step, 4)
        return tuple(at)

    def barrier(self):
        sem = pltpu.get_barrier_semaphore()
        pl.semaphore_signal(sem, inc=1, device_id=self.device(self.at, 1 - self.core), device_id_type=MESH)
        for d in (1, 2, 3):
            pl.semaphore_signal(sem, inc=1, device_id=self.device(self.moved(2, d), self.core), device_id_type=MESH)
        for i in range(1, 16):
            pl.semaphore_signal(sem, inc=1, device_id=self.plane_peer(i), device_id_type=MESH)
        pl.semaphore_wait(sem, 19)

    def plane_peer(self, i):
        chip = lax.rem(self.at[1] * 4 + self.at[0] + i, 16)
        return (chip * 2 + self.core, self.at[2])

    def bias_copy(self, bias, sems, d):
        ref = bias.at[self.at[2]]
        return pltpu.make_async_remote_copy(src_ref=ref, dst_ref=ref, send_sem=sems.at[0, d - 1], recv_sem=sems.at[1, d - 1],
            device_id=self.device(self.moved(2, d), self.core), device_id_type=MESH)

    def cols(self, core):
        return pl.ds(pl.multiple_of(core * 384, 128), 384)

    def pre(self, g):
        return pltpu.make_async_remote_copy(
            src_ref=self.stage.at[g], dst_ref=self.other.at[g], send_sem=self.psem.at[0, g], recv_sem=self.psem.at[1, g],
            device_id=self.device(self.at, 1 - self.core), device_id_type=MESH)

    def assemble(self, g):
        c = self.cols(self.core)
        mine, theirs = self.stage[g, :, c], self.other[g, :, c]
        first = self.core == 0
        both = jnp.concatenate([jnp.where(first, mine, theirs), jnp.where(first, theirs, mine)], axis=0).astype(BF)
        x, y, z = self.at
        for p in range(3):
            self.G[g, z, y, x, p, :, c] = both[p * 16:(p + 1) * 16]

    def view(self, g, p, phase, at, core):
        order = ORDERS[p]
        where = list(at)
        for axis in order[:phase]:
            where[axis] = slice(None)
        return self.G.at[g, where[2], where[1], where[0], p, :, self.cols(core)]

    def copy(self, g, p, phase, d):
        axis = ORDERS[p][phase]
        ref = self.view(g, p, phase, self.at, self.core)
        i = p * 9 + phase * 3 + d - 1
        return pltpu.make_async_remote_copy(
            src_ref=ref, dst_ref=ref, send_sem=self.ssem.at[g, i], recv_sem=self.rsem.at[g, i],
            device_id=self.device(self.moved(axis, d), self.core), device_id_type=MESH)

    def start(self, g, phase):
        for d in (1, 3, 2):
            for p in range(3):
                self.copy(g, p, phase, d).start()

    def arrive(self, g, phase):
        for d in (1, 3, 2):
            for p in range(3):
                self.copy(g, p, phase, d).wait_recv()

    def sent(self, g):
        for phase in range(3):
            for d in (1, 2, 3):
                for p in range(3):
                    self.copy(g, p, phase, d).wait_send()

    def pass_on(self, g, p, d):
        at = self.moved(ORDERS[p][2], 4 - d)
        ref = self.view(g, p, 2, at, self.core)
        return pltpu.make_async_remote_copy(
            src_ref=ref, dst_ref=ref, send_sem=self.fsem.at[g, p * 4 + d], recv_sem=self.gsem.at[g, p * 4 + d],
            device_id=self.device(self.at, 1 - self.core), device_id_type=MESH)

    def forward_own(self, g):
        for p in range(3):
            self.pass_on(g, p, 0).start()

    def forward(self, g):
        for d in (1, 3, 2):
            for p in range(3):
                self.copy(g, p, 2, d).wait_recv()
                self.pass_on(g, p, d).start()

    def finish(self, g):
        for d in range(4):
            for p in range(3):
                self.pass_on(g, p, d).wait_recv()

    def drain(self, g):
        for d in range(4):
            for p in range(3):
                self.pass_on(g, p, d).wait_send()


def compute(rows, lens, tok, table, trows, g1_, b1_, ob_, g2_, b2_, db_, cot, qvb, upb, wq, wo, wu, wd,
            out, tgrad, pgrad,
            inp, fin, qkv, probs, att, mid, sin, hid, dup, dmid, dml, dat, dqkv,
            G, stage, other, psem, ssem, rsem, fsem, gsem, bias, bsem,
            part, half, slots, zslots, final, rs_s, rs_r, zs, ag_s, ag_r, sb):
    t = lax.axis_index("tensor")
    row = lambda ref: ref[...].reshape(1, D)
    g1, b1, ob, g2, b2, db = (row(r) for r in (g1_, b1_, ob_, g2_, b2_, db_))
    net = Gather(G, stage, other, psem, ssem, rsem, fsem, gsem)
    stage[0] = jnp.concatenate([wq[0], wq[1], wq[2], wo[...]], axis=1)
    stage[1] = wu[...]
    stage[2] = wd[...]
    bias[t] = jnp.concatenate([qvb[0:1, :], jnp.zeros((1, QW), F32), qvb[1:2, :], jnp.zeros((1, 64), F32), upb[...].reshape(1, FZ)], axis=1)
    net.barrier()
    for d in (1, 2, 3):
        net.bias_copy(bias, bsem, d).start()
    for g in range(3):
        net.pre(g).start()
    for g in range(3):
        net.pre(g).wait_recv()
        net.assemble(g)
        net.start(g, 0)
    for g in range(3):
        net.arrive(g, 0)
        net.start(g, 1)
    for g in range(3):
        net.arrive(g, 1)
        net.start(g, 2)
        net.forward_own(g)
    for g in range(3):
        net.forward(g)
    for d in (1, 2, 3):
        net.bias_copy(bias, bsem, d).wait()
    for g in range(3):
        net.finish(g)
    load = lambda g, z: G[g, z].reshape(768, 768)
    wqkv = lambda z: load(0, z)[:, :576]
    wout = lambda z: load(0, z)[:, 576:]
    images = rows // SEQ
    hots = []
    for i in range(images):
        base = jnp.concatenate([trows[pl.ds(t * images + i, 1), :], jnp.full((1, 384 - PROMPTS), -1, jnp.int32)], axis=1)
        slot = pltpu.roll(base, PATCHES, 1)
        slot = slot[:, :SEQ]
        place = lax.broadcasted_iota(jnp.int32, (1, SEQ), 1)
        live = (place >= PATCHES) & (place < PATCHES + lens[t * images + i])
        slot = jnp.where(live, slot, -1)
        prow = lax.broadcasted_iota(jnp.int32, (PROMPTS, SEQ), 0)
        hots.append((prow == slot).astype(F32))
    for i in range(images):
        place = lax.broadcasted_iota(jnp.int32, (SEQ, 1), 0)
        live = (place >= PATCHES) & (place < PATCHES + lens[t * images + i])
        picked = lax.dot_general(hots[i], table[...], TN, precision=lax.Precision.HIGHEST, preferred_element_type=F32)
        inp[pl.ds(i * SEQ, SEQ), :] = jnp.where(live, picked, tok[pl.ds(i * SEQ, SEQ), :].astype(F32))

    @pl.loop(0, rows // CH)
    def _(c):
        sl = pl.ds(pl.multiple_of(c * CH, CH), CH)
        n, _ = stats(inp[sl, :])
        fin[sl, :] = (n * g1 + b1).astype(BF)

    @pl.loop(0, NZ)
    def _(z):
        x = mm(fin[...], wqkv(z))
        qkv[z] = (x + bias[z, :, 0:576]).astype(BF)

    @pl.loop(0, NZ)
    def _(z):
        for i in range(images):
            rs = pl.ds(i * SEQ, SEQ)
            blk = qkv[z, rs, :]
            place = lax.broadcasted_iota(jnp.int32, (1, SEQ), 1)
            bias = jnp.where(place < PATCHES + lens[t * images + i], 0.0, MASKED)
            outs = []
            for h in range(HZ):
                q = blk[:, h * HD:(h + 1) * HD] * 0.125
                k = blk[:, QW + h * HD:QW + (h + 1) * HD]
                v = blk[:, 2 * QW + h * HD:2 * QW + (h + 1) * HD]
                s = mm(q.astype(BF), k, NT) + bias
                m = jnp.max(s, axis=-1, keepdims=True)
                e = jnp.exp(s - m)
                p = (e / jnp.sum(e, axis=-1, keepdims=True)).astype(BF)
                probs[z, i * HZ + h] = p
                outs.append(mm(p, v).astype(BF))
            att[z, rs, :] = jnp.concatenate(outs, axis=1)

    @pl.loop(0, images)
    def _(i):
        rs = pl.ds(pl.multiple_of(i * SEQ, SEQ), SEQ)
        acc = mm(att[0, rs, :], wout(0), NT)
        for z in range(1, NZ):
            acc += mm(att[z, rs, :], wout(z), NT)
        mid[rs, :] = inp[rs, :] + acc + ob

    @pl.loop(0, rows // CH)
    def _(c):
        sl = pl.ds(pl.multiple_of(c * CH, CH), CH)
        n, _ = stats(mid[sl, :])
        sin[sl, :] = (n * g2 + b2).astype(BF)

    TF = 256
    NF = FZ // TF

    @pl.loop(0, NZ * NF)
    def _(j):
        z = j // NF
        f = pl.ds(pl.multiple_of((j % NF) * TF, TF), TF)
        fo = pl.ds(pl.multiple_of(j * TF, TF), TF)
        for i in range(images):
            rs = pl.ds(i * SEQ, SEQ)
            u = mm(sin[rs, :], G[1, z, :, :, :, :, f].reshape(768, TF)) + bias[z, :, pl.ds(pl.multiple_of(640 + (j % NF) * TF, 128), TF)]
            dh = mm(cot[rs, :], G[2, z, :, :, :, :, f].reshape(768, TF))
            a, b = gelu_pair(u)
            hid[rs, fo] = a.astype(BF)
            dup[rs, fo] = (dh * b).astype(BF)

    @pl.loop(0, images)
    def _(i):
        rs = pl.ds(pl.multiple_of(i * SEQ, SEQ), SEQ)
        acc = mm(hid[rs, 0:FZ], load(2, 0), NT)
        for z in range(1, NZ):
            acc += mm(hid[rs, z * FZ:(z + 1) * FZ], load(2, z), NT)
        out[rs, :] = (mid[rs, :] + acc + db).astype(BF)

    @pl.loop(0, images)
    def _(i):
        rs = pl.ds(pl.multiple_of(i * SEQ, SEQ), SEQ)
        acc = mm(dup[rs, 0:FZ], load(1, 0), NT)
        for z in range(1, NZ):
            acc += mm(dup[rs, z * FZ:(z + 1) * FZ], load(1, z), NT)
        dmid[rs, :] = acc

    @pl.loop(0, rows // CH)
    def _(c):
        sl = pl.ds(pl.multiple_of(c * CH, CH), CH)
        n, r = stats(mid[sl, :])
        d = cot[sl, :].astype(F32) + norm_back(dmid[sl, :], n, r, g2)
        dmid[sl, :] = d
        dml[sl, :] = d.astype(BF)

    @pl.loop(0, NZ)
    def _(z):
        dat[z] = mm(dml[...], wout(z)).astype(BF)

    @pl.loop(0, NZ)
    def _(z):
        for i in range(images):
            rs = pl.ds(i * SEQ, SEQ)
            blk = qkv[z, rs, :]
            dab = dat[z, rs, :]
            dq, dk, dv = [], [], []
            for h in range(HZ):
                q = blk[:, h * HD:(h + 1) * HD]
                k = blk[:, QW + h * HD:QW + (h + 1) * HD]
                v = blk[:, 2 * QW + h * HD:2 * QW + (h + 1) * HD]
                do = dab[:, h * HD:(h + 1) * HD]
                p = probs[z, i * HZ + h]
                dp = mm(do, v, NT)
                dv.append(mm(p, do, TN).astype(BF))
                pf = p.astype(F32)
                x = dp * pf
                ds = (x - pf * jnp.sum(x, axis=-1, keepdims=True)).astype(BF)
                dq.append((mm(ds, k) * 0.125).astype(BF))
                dk.append((mm(ds, q, TN) * 0.125).astype(BF))
            dqkv[z, rs, :] = jnp.concatenate(dq + dk + dv, axis=1)

    @pl.loop(0, images)
    def _(i):
        rs = pl.ds(pl.multiple_of(i * SEQ, SEQ), SEQ)
        acc = mm(dqkv[0, rs, :], wqkv(0), NT)
        for z in range(1, NZ):
            acc += mm(dqkv[z, rs, :], wqkv(z), NT)
        tgrad[rs, :] = acc

    @pl.loop(0, rows // CH)
    def _(c):
        sl = pl.ds(pl.multiple_of(c * CH, CH), CH)
        n, r = stats(inp[sl, :])
        d = dmid[sl, :] + norm_back(tgrad[sl, :], n, r, g1)
        tgrad[sl, :] = d

    total = None
    for i in range(images):
        rs = pl.ds(i * SEQ, SEQ)
        place = lax.broadcasted_iota(jnp.int32, (SEQ, 1), 0)
        live = (place >= PATCHES) & (place < PATCHES + lens[t * images + i])
        d = tgrad[rs, :]
        piece = lax.dot_general(hots[i], d, NN, precision=lax.Precision.HIGHEST, preferred_element_type=F32)
        total = piece if total is None else total + piece
        tgrad[rs, :] = jnp.where(live, 0.0, d)
    part[...] = jnp.concatenate([total, jnp.zeros((128 - PROMPTS, D), F32)], axis=0)

    core, chip = net.core, net.at[1] * 4 + net.at[0]
    mine, theirs = net.cols(core), net.cols(1 - core)
    swap = pltpu.make_async_remote_copy(src_ref=part.at[:, theirs], dst_ref=half, send_sem=sb.at[0], recv_sem=sb.at[1],
                                        device_id=net.device(net.at, 1 - core), device_id_type=MESH)
    swap.start()
    swap.wait()
    part[:, mine] = part[:, mine] + half[...]

    def scatter(i):
        dst = lax.rem(chip + i, 16)
        return pltpu.make_async_remote_copy(src_ref=part.at[pl.ds(pl.multiple_of(dst * 8, 8), 8), mine], dst_ref=slots.at[i],
                                            send_sem=rs_s.at[i], recv_sem=rs_r.at[i], device_id=net.plane_peer(i), device_id_type=MESH)
    for i in range(1, 16):
        scatter(i).start()
    here = pl.ds(pl.multiple_of(chip * 8, 8), 8)
    acc = part[here, mine]
    for i in range(1, 16):
        scatter(i).wait_recv()
        acc = acc + slots[i]
    zslots[t] = acc

    def zcopy(d):
        return pltpu.make_async_remote_copy(src_ref=zslots.at[t], dst_ref=zslots.at[t], send_sem=zs.at[0, d], recv_sem=zs.at[1, d],
                                            device_id=net.device(net.moved(2, d), core), device_id_type=MESH)
    for d in (1, 2, 3):
        zcopy(d).start()
    for d in (1, 2, 3):
        zcopy(d).wait()
    final[here, mine] = (zslots[0] + zslots[1]) + (zslots[2] + zslots[3])

    def spread(i):
        ref = final.at[here, mine]
        return pltpu.make_async_remote_copy(src_ref=ref, dst_ref=ref, send_sem=ag_s.at[i], recv_sem=ag_r.at[i],
                                            device_id=net.plane_peer(i), device_id_type=MESH)
    for i in range(1, 16):
        spread(i).start()
    for i in range(1, 16):
        spread(i).wait_recv()
    last = pltpu.make_async_remote_copy(src_ref=final.at[:, mine], dst_ref=final.at[:, mine], send_sem=sb.at[2], recv_sem=sb.at[3],
                                        device_id=net.device(net.at, 1 - core), device_id_type=MESH)
    last.start()
    last.wait()
    pgrad[...] = final[0:PROMPTS, :]
    for i in range(1, 16):
        scatter(i).wait_send()
        spread(i).wait_send()
    for g in range(3):
        net.sent(g)
        net.drain(g)
        net.pre(g).wait_send()


def body(tokens, prompt_table, lengths, table_rows, ln1_gain, ln1_bias, w_qkv, qv_bias, w_out, out_bias,
         ln2_gain, ln2_bias, w_up, up_bias, w_down, down_bias, cotangent):
    rows = tokens.shape[0]
    V = pl.BlockSpec(memory_space=pltpu.VMEM)
    S = pl.BlockSpec(memory_space=pltpu.SMEM)
    images = rows // SEQ
    DMA = pltpu.SemaphoreType.DMA
    return pl.pallas_call(
        functools.partial(compute, rows),
        out_shape=(jax.ShapeDtypeStruct((rows, D), BF), jax.ShapeDtypeStruct((rows, D), F32), jax.ShapeDtypeStruct((PROMPTS, D), F32)),
        in_specs=[S] + [V] * 16,
        out_specs=(V, V, V),
        scratch_shapes=[
            pltpu.VMEM((rows, D), F32),
            pltpu.VMEM((rows, D), BF),
            pltpu.VMEM((NZ, rows, 3 * QW), BF),
            pltpu.VMEM((NZ, images * HZ, SEQ, SEQ), BF),
            pltpu.VMEM((NZ, rows, QW), BF),
            pltpu.VMEM((rows, D), F32),
            pltpu.VMEM((rows, D), BF),
            pltpu.VMEM((rows, NZ * FZ), BF),
            pltpu.VMEM((rows, NZ * FZ), BF),
            pltpu.VMEM((rows, D), F32),
            pltpu.VMEM((rows, D), BF),
            pltpu.VMEM((NZ, rows, QW), BF),
            pltpu.VMEM((NZ, rows, 3 * QW), BF),
            pltpu.VMEM((3, 4, 4, 4, 3, 16, 768), BF),
            pltpu.VMEM((3, 24, 768), F32), pltpu.VMEM((3, 24, 768), F32),
            DMA((2, 3)), DMA((3, 27)), DMA((3, 27)), DMA((3, 12)), DMA((3, 12)),
            pltpu.VMEM((NZ, 1, 1408), F32), DMA((2, 3)),
            pltpu.VMEM((128, D), F32), pltpu.VMEM((128, 384), F32), pltpu.VMEM((16, 8, 384), F32), pltpu.VMEM((4, 8, 384), F32),
            pltpu.VMEM((128, D), F32),
            DMA((16,)), DMA((16,)), DMA((2, 4)), DMA((16,)), DMA((16,)), DMA((4,)),
        ],
        compiler_params=pltpu.CompilerParams(collective_id=1, has_side_effects=True, vmem_limit_bytes=62 * 2**20),
    )(lengths, tokens, prompt_table, table_rows, ln1_gain, ln1_bias, out_bias, ln2_gain, ln2_bias, down_bias, cotangent,
      qv_bias, up_bias, w_qkv, w_out.T, w_up, w_down.T)


def solution(mesh):
    row = P(("dp", "tensor"), None)
    return jax.shard_map(
        body, mesh=mesh,
        in_specs=(row, P(), P("dp"), P("dp", None), P(), P(), P(None, "dp", "tensor"), P(None, "tensor"), P("tensor", "dp"),
                  P(), P(), P(), P("dp", "tensor"), P("tensor"), P("tensor", "dp"), P(), row),
        out_specs=(row, row, P()), check_vma=False)
```

```python
import functools

import jax
import jax.numpy as jnp
from jax import lax
from jax.experimental import pallas as pl
from jax.experimental.pallas import tpu as pltpu
from jax.sharding import PartitionSpec as P

D = 768
HD = 64
PATCHES = 197
PROMPTS = 100
SEQ = 304
NZ = 4
HZ = 3
QW = 192
FZ = 768
EPSILON = 1e-06
MASKED = -1e30
F32 = jnp.float32
BF = jnp.bfloat16
NN = (((1,), (0,)), ((), ()))
NT = (((1,), (1,)), ((), ()))
TN = (((0,), (0,)), ((), ()))
MESH = pl.DeviceIdType.MESH
DMA = pltpu.SemaphoreType.DMA
ORDERS = ((0, 1, 2), (1, 2, 0), (2, 0, 1))
NEAR_FIRST = (1, 3, 2)
TAIL = 192


def mm(a, b, dims=NN):
    return lax.dot_general(a, b, dims, preferred_element_type=F32)


def exact(a, b, dims=NN):
    return lax.dot_general(a, b, dims, precision=lax.Precision.HIGHEST, preferred_element_type=F32)


def gelu_pair(u):
    t = 1.0 / (1.0 + (0.3275911 * 0.7071067811865476) * jnp.abs(u))
    e = jnp.exp(-0.5 * (u * u))
    poly = t * (0.254829592 + t * (-0.284496736 + t * (1.421413741 + t * (-1.453152027 + t * 1.061405429))))
    half = 0.5 * poly * e
    cdf = jnp.where(u >= 0, 1.0 - half, half)
    return u * cdf, cdf + u * (0.3989422804014327 * e)


def stats(h):
    c = h - jnp.mean(h, axis=-1, keepdims=True)
    r = lax.rsqrt(jnp.mean(c * c, axis=-1, keepdims=True) + EPSILON)
    return c * r, r


def norm_back(g, n, r, gain):
    e = g * gain
    return r * (e - jnp.mean(e, axis=-1, keepdims=True) - n * jnp.mean(e * n, axis=-1, keepdims=True))


class Net:
    def __init__(self):
        dp = lax.axis_index("dp")
        self.core = lax.rem(dp, 2)
        self.chip = lax.div(dp, 2)
        self.at = (lax.rem(self.chip, 4), lax.div(self.chip, 4), lax.axis_index("tensor"))

    def device(self, at, core):
        return ((at[1] * 4 + at[0]) * 2 + core, at[2])

    def moved(self, axis, step):
        at = list(self.at)
        at[axis] = lax.rem(at[axis] + step, 4)
        return tuple(at)

    def sibling(self):
        return self.device(self.at, 1 - self.core)

    def along(self, axis, step):
        return self.device(self.moved(axis, step), self.core)

    def plane(self, i):
        return (lax.rem(self.chip + i, 16) * 2 + self.core, self.at[2])

    def greet(self):
        sem = pltpu.get_barrier_semaphore()
        peers = [self.sibling()] + [self.plane(i) for i in range(1, 16)] + [self.along(2, d) for d in (1, 2, 3)]
        for peer in peers:
            pl.semaphore_signal(sem, inc=1, device_id=peer, device_id_type=MESH)
        return len(peers)


def remote(src, dst, send, recv, to):
    return pltpu.make_async_remote_copy(src_ref=src, dst_ref=dst, send_sem=send, recv_sem=recv, device_id=to, device_id_type=MESH)


class Part:
    def __init__(self, net, G, mats, first, width, sems, base):
        self.net, self.G, self.mats, self.sems, self.base = net, G, mats, sems, base
        self.cols = pl.ds(pl.multiple_of(first + net.core * width, 128), width)

    def view(self, p, phase, at, cols):
        where = list(at)
        for axis in ORDERS[p][:phase]:
            where[axis] = slice(None)
        return self.G.at[self.mats, where[2], where[1], where[0], p, :, cols]

    def copy(self, p, phase, d, send, recv, cols=None):
        ref = self.view(p, phase, self.net.at, self.cols if cols is None else cols)
        return remote(ref, ref, self.sems.at[send], self.sems.at[recv], self.net.along(ORDERS[p][phase], d))

    def start(self, phase, send, recv, ds=NEAR_FIRST, cols=None):
        for d in ds:
            for p in range(3):
                self.copy(p, phase, d, send, recv, cols).start()

    def bulk(self, blocks, cols=None):
        cols = self.cols if cols is None else cols
        if blocks == 9:
            return self.G.at[self.mats, 0, 0, 0:3, :, :, cols]
        if blocks == 36:
            return self.G.at[self.mats, 0, :, 0:3, :, :, cols]
        if blocks == 48:
            return self.G.at[self.mats, 0, :, :, :, :, cols]
        if blocks == 144:
            return self.G.at[self.mats, :, :, 0:3, :, :, cols]
        return self.G.at[self.mats, :, :, :, :, :, cols]

    def wait(self, blocks, sem, cols=None):
        ref = self.bulk(blocks, cols)
        remote(ref, ref, self.sems.at[sem], self.sems.at[sem], self.net.sibling()).wait_recv()

    def slab(self, p, d, send, recv, cols=None):
        at = self.net.moved(ORDERS[p][2], 4 - d) if d else self.net.at
        ref = self.view(p, 2, at, self.cols if cols is None else cols)
        return remote(ref, ref, self.sems.at[send], self.sems.at[recv], self.net.sibling())

    def tile(self, p, send, recv, cols=None):
        ref = self.G.at[self.mats, :, :, :, p, :, self.cols if cols is None else cols]
        return remote(ref, ref, self.sems.at[send], self.sems.at[recv], self.net.sibling())


def compute(rows, lens_h, tok_h, table_h, trows_h, g1_h, b1_h, ob_h, g2_h, b2_h, db_h, cot_h, qvb_h, upb_h, wq_h, wo_h, wu_h, wd_h,
            out_h, tgrad_h, pgrad_h,
            lens, tok, table, trows, g1_, b1_, ob_, g2_, b2_, db_, cot, qvb, upb, wq, wo, wu, wd,
            inp, fin, qkv, probs, att, mid, sin, hid, dup, dmid, dml, dat, dqkv, out, tgrad,
            G, stage, other, bias, part, half, slots, zslots, final, isem, psem, gsem, tsem, osem):
    images = rows // SEQ
    net = Net()
    t = net.at[2]
    n_peers = net.greet()

    loads = []
    for k, (src, dst) in enumerate(((wq_h, wq), (wo_h, wo), (wu_h, wu), (wd_h, wd), (lens_h, lens), (trows_h, trows), (table_h, table),
                                    (tok_h, tok), (qvb_h, qvb), (upb_h, upb), (g1_h, g1_), (b1_h, b1_), (ob_h, ob_), (g2_h, g2_),
                                    (b2_h, b2_), (db_h, db_), (cot_h, cot))):
        loads.append(pltpu.make_async_copy(src, dst, isem.at[k]))
    for load in loads:
        load.start()
    for load in loads[:4]:
        load.wait()
    stage[0] = jnp.concatenate([wq[0], wq[1], wq[2], wo[...]], axis=1)
    stage[1] = wu[...]
    stage[2] = wd[...]
    for load in loads[4:12]:
        load.wait()

    hots, lives = [], []
    for i in range(images):
        length = lens[t * images + i]
        base = jnp.concatenate([trows[pl.ds(t * images + i, 1), :], jnp.full((1, 384 - PROMPTS), -1, jnp.int32)], axis=1)
        slot = pltpu.roll(base, PATCHES - TAIL, 1)[:, :SEQ - TAIL]
        place = lax.broadcasted_iota(jnp.int32, (1, SEQ - TAIL), 1) + TAIL
        slot = jnp.where((place >= PATCHES) & (place < PATCHES + length), slot, -1)
        hots.append((lax.broadcasted_iota(jnp.int32, (PROMPTS, SEQ - TAIL), 0) == slot).astype(F32))
        place = lax.broadcasted_iota(jnp.int32, (SEQ - TAIL, 1), 0) + TAIL
        lives.append((place >= PATCHES) & (place < PATCHES + length))
    row = lambda ref: ref[...].reshape(1, D)
    for i in range(images):
        lo, hi = pl.ds(i * SEQ, TAIL), pl.ds(i * SEQ + TAIL, SEQ - TAIL)
        inp[lo, :] = tok[lo, :].astype(F32)
        inp[hi, :] = jnp.where(lives[i], exact(hots[i], table[...], TN), tok[hi, :].astype(F32))
        rs = pl.ds(i * SEQ, SEQ)
        fin[rs, :] = (stats(inp[rs, :])[0] * row(g1_) + row(b1_)).astype(BF)
    bias[t] = jnp.concatenate([qvb[0:1, :], jnp.zeros((1, QW), F32), qvb[1:2, :], jnp.zeros((1, 64), F32), upb[...].reshape(1, FZ)], axis=1)

    a = Part(net, G, 0, 0, 256, gsem, 0)
    b = Part(net, G, 0, 512, 128, gsem, 0)
    c = Part(net, G, slice(1, 3), 0, 384, gsem, 0)
    sub = [pl.ds(pl.multiple_of(net.core * 384 + 128 * j, 128), 128) for j in range(3)]
    pl.semaphore_wait(pltpu.get_barrier_semaphore(), n_peers)

    def pre(m):
        return remote(stage.at[m], other.at[m], psem.at[0, m], psem.at[1, m], net.sibling())

    def assemble(m, first, width):
        cs = pl.ds(pl.multiple_of(first + net.core * width, 128), width)
        mine, theirs = stage[m, :, cs], other[m, :, cs]
        own = net.core == 0
        both = jnp.concatenate([jnp.where(own, mine, theirs), jnp.where(own, theirs, mine)], axis=0).astype(BF)
        x, y, z = net.at
        for p in range(3):
            G[m, z, y, x, p, :, cs] = both[p * 16:(p + 1) * 16]

    def bias_copy(d):
        return remote(bias.at[t], bias.at[t], psem.at[0, 3], psem.at[1, 3], net.along(2, d))

    for m in range(3):
        pre(m).start()
    pre(0).wait_recv()
    assemble(0, 0, 256)
    a.start(0, 0, 1)
    assemble(0, 512, 128)
    b.start(0, 2, 3)
    for m in (1, 2):
        pre(m).wait_recv()
        assemble(m, 0, 384)
    c.start(0, 4, 5)
    for d in (1, 2, 3):
        bias_copy(d).start()
    a.wait(9, 1)
    a.start(1, 6, 7)
    b.wait(9, 3)
    b.start(1, 8, 9)
    c.wait(9, 5)
    c.start(1, 10, 11)
    a.wait(36, 7)
    for d, r in zip(NEAR_FIRST, (13, 14, 15)):
        a.start(2, 12, r, (d,))
    for p in range(3):
        a.slab(p, 0, 16, 17).start()
    b.wait(36, 9)
    b.start(2, 18, 19)
    c.wait(36, 11)
    for j in range(3):
        c.start(2, 22 + 4 * j, 23 + 4 * j, NEAR_FIRST, sub[j])
    for d, r in zip(NEAR_FIRST, (13, 14, 15)):
        a.wait(48, r)
        for p in range(3):
            a.slab(p, d, 16, 17).start()
    other_a = Part(net, G, 0, 0, 256, gsem, 0)
    a.wait(192, 17)
    remote(bias.at[pl.ds(0, 3)], bias.at[pl.ds(0, 3)], psem.at[0, 3], psem.at[1, 3], net.sibling()).wait()

    def load(m, z, lo, hi):
        return G[m, z, :, :, :, :, lo:hi].reshape(D, hi - lo)

    x = fin[...]
    for z in range(NZ):
        qkv[z, :, 0:512] = (mm(x, load(0, z, 0, 512)) + bias[z, :, 0:512]).astype(BF)
    b.wait(144, 19)
    for p in range(3):
        b.tile(p, 20, 21).start()
    b.wait(192, 21)
    last = mm(fin[...], jnp.concatenate([load(0, z, 512, 576) for z in range(NZ)], axis=1))
    for z in range(NZ):
        qkv[z, :, 512:576] = (last[:, z * 64:(z + 1) * 64] + bias[z, :, 512:576]).astype(BF)

    def attend(z):
        for i in range(images):
            rs = pl.ds(i * SEQ, SEQ)
            blk = qkv[z, rs, :]
            alive = lax.broadcasted_iota(jnp.int32, (SEQ - TAIL, 1), 0) + TAIL < PATCHES + lens[t * images + i]
            outs = []
            for h in range(HZ):
                q = (blk[:, h * HD:(h + 1) * HD] * 0.125).astype(BF)
                k = blk[:, QW + h * HD:QW + (h + 1) * HD]
                v = blk[:, 2 * QW + h * HD:2 * QW + (h + 1) * HD]
                s = mm(k, q, NT)
                s = jnp.concatenate([s[:TAIL], jnp.where(alive, s[TAIL:], MASKED)], axis=0)
                e = jnp.exp(s - jnp.max(s, axis=0, keepdims=True))
                p = (e * (1.0 / jnp.sum(e, axis=0, keepdims=True))).astype(BF)
                probs[z, i * HZ + h] = p
                outs.append(mm(p, v, TN).astype(BF))
            att[rs, z * QW:(z + 1) * QW] = jnp.concatenate(outs, axis=1)

    def relay(j):
        c.wait(144, 23 + 4 * j, sub[j])
        for p in range(3):
            c.tile(p, 24 + 4 * j, 25 + 4 * j, sub[j]).start()

    attend(0)
    attend(1)
    attend(2)
    relay(0)
    attend(3)

    for load_ in loads[12:]:
        load_.wait()
    wout = jnp.concatenate([load(0, z, 576, 768) for z in range(NZ)], axis=1)
    for i in range(images):
        rs = pl.ds(i * SEQ, SEQ)
        h = inp[rs, :] + mm(att[rs, :], wout, NT) + row(ob_)
        mid[rs, :] = h
        sin[rs, :] = (stats(h)[0] * row(g2_) + row(b2_)).astype(BF)

    def pair(m, z, j):
        return jnp.concatenate([load(m, z, j * 128, (j + 1) * 128), load(m, z, 384 + j * 128, 512 + j * 128)], axis=1)

    def third(j):
        c.wait(192, 25 + 4 * j, sub[j])
        for z in range(NZ):
            n = j * NZ + z
            ub = jnp.concatenate([bias[z, :, 640 + j * 128:768 + j * 128], bias[z, :, 1024 + j * 128:1152 + j * 128]], axis=1)
            u = mm(sin[...], pair(1, z, j)) + ub
            dh = mm(cot[...], pair(2, z, j))
            g, slope = gelu_pair(u)
            hid[:, n * 256:(n + 1) * 256] = g.astype(BF)
            dup[:, n * 256:(n + 1) * 256] = (dh * slope).astype(BF)

    def second(j):
        w = jnp.concatenate([pair(1, z, j) for z in range(NZ)], axis=1)
        return mm(dup[:, j * 1024:(j + 1) * 1024], w, NT)

    third(0)
    relay(1)
    dmid[...] = second(0)
    third(1)
    relay(2)
    dmid[...] += second(1)
    third(2)
    dmid[...] += second(2)

    for i in range(images):
        rs = pl.ds(i * SEQ, SEQ)
        n, r = stats(mid[rs, :])
        d = cot[rs, :].astype(F32) + norm_back(dmid[rs, :], n, r, row(g2_))
        dmid[rs, :] = d
        dml[rs, :] = d.astype(BF)
    wout = jnp.concatenate([load(0, z, 576, 768) for z in range(NZ)], axis=1)
    dat[...] = mm(dml[...], wout).astype(BF)

    for z in range(NZ):
        for i in range(images):
            rs = pl.ds(i * SEQ, SEQ)
            blk = qkv[z, rs, :]
            dab = dat[rs, z * QW:(z + 1) * QW]
            kt = blk[:, QW:2 * QW].T
            dq, dk, dv = [], [], []
            for h in range(HZ):
                q = blk[:, h * HD:(h + 1) * HD]
                v = blk[:, 2 * QW + h * HD:2 * QW + (h + 1) * HD]
                do = dab[:, h * HD:(h + 1) * HD]
                p = probs[z, i * HZ + h]
                dv.append(mm(p, do).astype(BF))
                pf = p.astype(F32)
                x = mm(v, do, NT) * pf
                ds = (x - pf * jnp.sum(x, axis=0, keepdims=True)).astype(BF)
                dk.append((mm(ds, q) * 0.125).astype(BF))
                dq.append(mm(kt[h * HD:(h + 1) * HD], ds))
            dq = (jnp.concatenate(dq, axis=0).T * 0.125).astype(BF)
            dqkv[rs, z * 3 * QW:(z + 1) * 3 * QW] = jnp.concatenate([dq] + dk + dv, axis=1)

    wqkv = jnp.concatenate([load(0, z, 0, 576) for z in range(NZ)], axis=1)
    total = None
    for i in range(images):
        hi = pl.ds(i * SEQ + TAIL, SEQ - TAIL)
        g = mm(dqkv[hi, :], wqkv, NT)
        n, r = stats(inp[hi, :])
        d = dmid[hi, :] + norm_back(g, n, r, row(g1_))
        tgrad[hi, :] = jnp.where(lives[i], 0.0, d)
        piece = exact(hots[i], d)
        total = piece if total is None else total + piece
    part[...] = jnp.concatenate([total, jnp.zeros((128 - PROMPTS, D), F32)], axis=0)

    core, chip = net.core, net.chip
    mine = pl.ds(pl.multiple_of(core * 384, 128), 384)
    theirs = pl.ds(pl.multiple_of((1 - core) * 384, 128), 384)
    here = pl.ds(pl.multiple_of(chip * 8, 8), 8)

    def rest(i):
        lo = pl.ds(i * SEQ, TAIL)
        w = jnp.concatenate([load(0, z, 0, 576) for z in range(NZ)], axis=1)
        n, r = stats(inp[lo, :])
        tgrad[lo, :] = dmid[lo, :] + norm_back(mm(dqkv[lo, :], w, NT), n, r, row(g1_))

    def down(i):
        rs = pl.ds(i * SEQ, SEQ)
        acc = None
        for j in range(3):
            w = jnp.concatenate([pair(2, z, j) for z in range(NZ)], axis=1)
            piece = mm(hid[rs, j * 1024:(j + 1) * 1024], w, NT)
            acc = piece if acc is None else acc + piece
        out[rs, :] = (mid[rs, :] + acc + row(db_)).astype(BF)

    swap = remote(part.at[:, theirs], half, tsem.at[0], tsem.at[1], net.sibling())
    swap.start()
    rest(0)
    swap.wait()
    part[:, mine] = part[:, mine] + half[...]
    for i in range(1, 16):
        dst = lax.rem(chip + i, 16)
        remote(part.at[pl.ds(pl.multiple_of(dst * 8, 8), 8), mine], slots.at[i], tsem.at[2], tsem.at[3], net.plane(i)).start()
    rest(1)
    tout = pltpu.make_async_copy(tgrad, tgrad_h, osem.at[0])
    tout.start()
    down(0)
    fifteen = slots.at[pl.ds(1, 15)]
    remote(fifteen, fifteen, tsem.at[2], tsem.at[3], net.sibling()).wait()
    acc = part[here, mine]
    for i in range(1, 16):
        acc = acc + slots[i]
    zslots[t] = acc
    for d in (1, 2, 3):
        remote(zslots.at[t], zslots.at[t], tsem.at[4], tsem.at[5], net.along(2, d)).start()
    down(1)
    oout = pltpu.make_async_copy(out, out_h, osem.at[1])
    oout.start()
    three = zslots.at[pl.ds(0, 3)]
    remote(three, three, tsem.at[4], tsem.at[5], net.sibling()).wait()
    final[here, mine] = (zslots[0] + zslots[1]) + (zslots[2] + zslots[3])
    ref = final.at[here, mine]
    for i in range(1, 16):
        remote(ref, ref, tsem.at[6], tsem.at[7], net.plane(i)).start()
    for m in range(3):
        pre(m).wait_send()
    for blocks, sem, pt in ((9, 0, a), (36, 6, a), (144, 12, a), (192, 16, a), (9, 2, b), (36, 8, b), (144, 18, b), (192, 20, b), (9, 4, c), (36, 10, c)):
        ref2 = pt.bulk(blocks)
        remote(ref2, ref2, gsem.at[sem], gsem.at[sem], net.sibling()).wait_send()
    for j in range(3):
        for blocks, sem in ((144, 22 + 4 * j), (192, 24 + 4 * j)):
            ref2 = c.bulk(blocks, sub[j])
            remote(ref2, ref2, gsem.at[sem], gsem.at[sem], net.sibling()).wait_send()
    many = final.at[pl.ds(0, 120), mine]
    remote(many, many, tsem.at[6], tsem.at[7], net.sibling()).wait()
    done = remote(final.at[pl.ds(0, 104), mine], final.at[pl.ds(0, 104), mine], tsem.at[8], tsem.at[9], net.sibling())
    done.start()
    done.wait()
    pout = pltpu.make_async_copy(final.at[pl.ds(0, 104)], pgrad_h, osem.at[2])
    pout.start()
    pout.wait()
    tout.wait()
    oout.wait()


def body(tokens, prompt_table, lengths, table_rows, ln1_gain, ln1_bias, w_qkv, qv_bias, w_out, out_bias,
         ln2_gain, ln2_bias, w_up, up_bias, w_down, down_bias, cotangent):
    rows = tokens.shape[0]
    images = rows // SEQ
    any_ = pl.BlockSpec(memory_space=pl.ANY)
    args = (lengths, tokens, prompt_table, table_rows, ln1_gain, ln1_bias, out_bias, ln2_gain, ln2_bias, down_bias, cotangent,
            qv_bias, up_bias, w_qkv, w_out.T, w_up, w_down.T)
    vmem = lambda shape, dtype: pltpu.VMEM(shape, dtype)
    token_out, grad_out, table_out = pl.pallas_call(
        functools.partial(compute, rows),
        out_shape=(jax.ShapeDtypeStruct((rows, D), BF), jax.ShapeDtypeStruct((rows, D), F32), jax.ShapeDtypeStruct((104, D), F32)),
        in_specs=[any_] * len(args),
        out_specs=(any_, any_, any_),
        scratch_shapes=[pltpu.SMEM(lengths.shape, lengths.dtype)] + [vmem(v.shape, v.dtype) for v in args[1:]] + [
            vmem((rows, D), F32),
            vmem((rows, D), BF),
            vmem((NZ, rows, 3 * QW), BF),
            vmem((NZ, images * HZ, SEQ, SEQ), BF),
            vmem((rows, D), BF),
            vmem((rows, D), F32),
            vmem((rows, D), BF),
            vmem((rows, NZ * FZ), BF),
            vmem((rows, NZ * FZ), BF),
            vmem((rows, D), F32),
            vmem((rows, D), BF),
            vmem((rows, D), BF),
            vmem((rows, 3 * D), BF),
            vmem((rows, D), BF),
            vmem((rows, D), F32),
            vmem((3, 4, 4, 4, 3, 16, 768), BF),
            vmem((3, 24, 768), F32),
            vmem((3, 24, 768), F32),
            vmem((NZ, 1, 1408), F32),
            vmem((128, D), F32),
            vmem((128, 384), F32),
            vmem((16, 8, 384), F32),
            vmem((NZ, 8, 384), F32),
            vmem((128, D), F32),
            DMA((len(args),)), DMA((2, 4)), DMA((34,)), DMA((10,)), DMA((3,)),
        ],
        compiler_params=pltpu.CompilerParams(collective_id=1, has_side_effects=True, vmem_limit_bytes=63 * 2**20),
    )(*args)
    return token_out, grad_out, table_out[:PROMPTS]


def solution(mesh):
    row = P(("dp", "tensor"), None)
    return jax.shard_map(
        body, mesh=mesh,
        in_specs=(row, P(), P("dp"), P("dp", None), P(), P(), P(None, "dp", "tensor"), P(None, "tensor"), P("tensor", "dp"),
                  P(), P(), P(), P("dp", "tensor"), P("tensor"), P("tensor", "dp"), P(), row),
        out_specs=(row, row, P()), check_vma=False)
```

```python
import functools

import jax
import jax.numpy as jnp
from jax import lax
from jax.experimental import pallas as pl
from jax.experimental.pallas import tpu as pltpu
from jax.sharding import PartitionSpec as P

D = 768
HD = 64
PATCHES = 197
PROMPTS = 100
SEQ = 304
NZ = 4
HZ = 3
QW = 192
FZ = 768
EPSILON = 1e-06
MASKED = -1e30
F32 = jnp.float32
BF = jnp.bfloat16
NN = (((1,), (0,)), ((), ()))
NT = (((1,), (1,)), ((), ()))
TN = (((0,), (0,)), ((), ()))
MESH = pl.DeviceIdType.MESH
DMA = pltpu.SemaphoreType.DMA
ORDERS = ((0, 1, 2), (1, 2, 0), (2, 0, 1))
NEAR_FIRST = (1, 3, 2)
TAIL = 192


def mm(a, b, dims=NN):
    return lax.dot_general(a, b, dims, preferred_element_type=F32)


def exact(a, b, dims=NN):
    return lax.dot_general(a, b, dims, precision=lax.Precision.HIGHEST, preferred_element_type=F32)


def gelu_pair(u):
    t = 1.0 / (1.0 + (0.3275911 * 0.7071067811865476) * jnp.abs(u))
    e = jnp.exp(-0.5 * (u * u))
    poly = t * (0.254829592 + t * (-0.284496736 + t * (1.421413741 + t * (-1.453152027 + t * 1.061405429))))
    half = 0.5 * poly * e
    cdf = jnp.where(u >= 0, 1.0 - half, half)
    return u * cdf, cdf + u * (0.3989422804014327 * e)


def stats(h):
    c = h - jnp.mean(h, axis=-1, keepdims=True)
    r = lax.rsqrt(jnp.mean(c * c, axis=-1, keepdims=True) + EPSILON)
    return c * r, r


def norm_back(g, n, r, gain):
    e = g * gain
    return r * (e - jnp.mean(e, axis=-1, keepdims=True) - n * jnp.mean(e * n, axis=-1, keepdims=True))


class Net:
    def __init__(self):
        dp = lax.axis_index("dp")
        self.core = lax.rem(dp, 2)
        self.chip = lax.div(dp, 2)
        self.at = (lax.rem(self.chip, 4), lax.div(self.chip, 4), lax.axis_index("tensor"))

    def device(self, at, core):
        return ((at[1] * 4 + at[0]) * 2 + core, at[2])

    def moved(self, axis, step):
        at = list(self.at)
        at[axis] = lax.rem(at[axis] + step, 4)
        return tuple(at)

    def sibling(self):
        return self.device(self.at, 1 - self.core)

    def along(self, axis, step):
        return self.device(self.moved(axis, step), self.core)

    def plane(self, i):
        return (lax.rem(self.chip + i, 16) * 2 + self.core, self.at[2])

    def greet(self):
        sem = pltpu.get_barrier_semaphore()
        peers = [self.sibling()] + [self.plane(i) for i in range(1, 16)] + [self.along(2, d) for d in (1, 2, 3)]
        for peer in peers:
            pl.semaphore_signal(sem, inc=1, device_id=peer, device_id_type=MESH)
        return len(peers)


def remote(src, dst, send, recv, to):
    return pltpu.make_async_remote_copy(src_ref=src, dst_ref=dst, send_sem=send, recv_sem=recv, device_id=to, device_id_type=MESH)


class Part:
    def __init__(self, net, G, where, sems):
        self.net, self.G, self.where, self.sems = net, G, where, sems

    def view(self, p, phase, at, half=None):
        at = list(at)
        for axis in ORDERS[p][:phase]:
            at[axis] = slice(None)
        if half is not None:
            at[ORDERS[p][0]] = pl.ds(2 * half, 2)
        return self.G.at[(*self.where, at[2], at[1], at[0], p)]

    def start(self, phase, send, recv, ds=NEAR_FIRST):
        for d in ds:
            for p in range(3):
                ref = self.view(p, phase, self.net.at)
                remote(ref, ref, self.sems.at[send], self.sems.at[recv], self.net.along(ORDERS[p][phase], d)).start()

    def pass_along(self, send, recv):
        for p in range(3):
            for d in (1, 3):
                axis = ORDERS[p][2]
                ref = self.view(p, 2, self.net.moved(axis, 4 - d), d // 2)
                remote(ref, ref, self.sems.at[send], self.sems.at[recv], self.net.along(axis, d)).start()

    def bulk(self, blocks):
        all_ = slice(None)
        piece = {9: (0, 0, pl.ds(0, 3)), 36: (0, all_, pl.ds(0, 3)), 48: (0,), 96: (pl.ds(0, 2),), 144: (all_, all_, pl.ds(0, 3)), 192: ()}[blocks]
        return self.G.at[(*self.where, *piece)]

    def wait(self, blocks, sem):
        ref = self.bulk(blocks)
        remote(ref, ref, self.sems.at[sem], self.sems.at[sem], self.net.sibling()).wait_recv()

    def wait_sent(self, blocks, sem):
        ref = self.bulk(blocks)
        remote(ref, ref, self.sems.at[sem], self.sems.at[sem], self.net.sibling()).wait_send()

    def slab(self, p, d, send, recv):
        ref = self.view(p, 2, self.net.moved(ORDERS[p][2], 4 - d) if d else self.net.at)
        return remote(ref, ref, self.sems.at[send], self.sems.at[recv], self.net.sibling())

    def whole(self, send, recv):
        ref = self.bulk(192)
        return remote(ref, ref, self.sems.at[send], self.sems.at[recv], self.net.sibling())


def compute(rows, lens_h, tok_h, table_h, trows_h, g1_h, b1_h, ob_h, g2_h, b2_h, db_h, cot_h, qvb_h, upb_h, wq_h, wo_h, wu_h, wd_h,
            out_h, tgrad_h, pgrad_h,
            lens, tok, table, trows, g1_, b1_, ob_, g2_, b2_, db_, cot, qvb, upb, wq, wo, wu, wd,
            inp, fin, qkv, probs, att, mid, sin, hid, dup, dmid, dml, dat, dqkv, out, tgrad,
            GA, GB, GC, stage, other, bias, part, half, slots, zslots, final, pbuf, isem, psem, gsem, tsem, osem):
    images = rows // SEQ
    net = Net()
    t = net.at[2]
    n_peers = net.greet()

    loads = []
    for k, (src, dst) in enumerate(((wq_h, wq), (wo_h, wo), (wu_h, wu), (wd_h, wd), (lens_h, lens), (trows_h, trows), (table_h, table),
                                    (tok_h, tok), (qvb_h, qvb), (upb_h, upb), (g1_h, g1_), (b1_h, b1_), (ob_h, ob_), (g2_h, g2_),
                                    (b2_h, b2_), (db_h, db_), (cot_h, cot))):
        loads.append(pltpu.make_async_copy(src, dst, isem.at[k]))
    for load in loads:
        load.start()
    for load in loads[:4]:
        load.wait()
    stage[0] = jnp.concatenate([wq[0], wq[1], wq[2], wo[...]], axis=1)
    stage[1] = wu[...]
    stage[2] = wd[...]
    for load in loads[4:12]:
        load.wait()

    hots, lives = [], []
    for i in range(images):
        length = lens[t * images + i]
        base = jnp.concatenate([trows[pl.ds(t * images + i, 1), :], jnp.full((1, 384 - PROMPTS), -1, jnp.int32)], axis=1)
        slot = pltpu.roll(base, PATCHES - TAIL, 1)[:, :SEQ - TAIL]
        place = lax.broadcasted_iota(jnp.int32, (1, SEQ - TAIL), 1) + TAIL
        slot = jnp.where((place >= PATCHES) & (place < PATCHES + length), slot, -1)
        hots.append((lax.broadcasted_iota(jnp.int32, (PROMPTS, SEQ - TAIL), 0) == slot).astype(F32))
        place = lax.broadcasted_iota(jnp.int32, (SEQ - TAIL, 1), 0) + TAIL
        lives.append((place >= PATCHES) & (place < PATCHES + length))
    row = lambda ref: ref[...].reshape(1, D)
    for i in range(images):
        lo, hi = pl.ds(i * SEQ, TAIL), pl.ds(i * SEQ + TAIL, SEQ - TAIL)
        inp[lo, :] = tok[lo, :].astype(F32)
        inp[hi, :] = jnp.where(lives[i], exact(hots[i], table[...], TN), tok[hi, :].astype(F32))
        rs = pl.ds(i * SEQ, SEQ)
        fin[rs, :] = (stats(inp[rs, :])[0] * row(g1_) + row(b1_)).astype(BF)
    bias[t] = jnp.concatenate([qvb[0:1, :], jnp.zeros((1, QW), F32), qvb[1:2, :], jnp.zeros((1, 64), F32), upb[...].reshape(1, FZ)], axis=1)

    a = Part(net, GA, (net.core,), gsem)
    b = Part(net, GB, (net.core,), gsem)
    c = Part(net, GC, (slice(None), net.core, slice(None)), gsem)

    def third(j):
        return Part(net, GC, (j, net.core, slice(None)), gsem)

    pl.semaphore_wait(pltpu.get_barrier_semaphore(), n_peers)

    def pre(m):
        return remote(stage.at[m], other.at[m], psem.at[0, m], psem.at[1, m], net.sibling())

    def assemble(m, G, where, first, width):
        cs = pl.ds(pl.multiple_of(first + net.core * width, 128), width)
        mine, theirs = stage[m, :, cs], other[m, :, cs]
        own = net.core == 0
        both = jnp.concatenate([jnp.where(own, mine, theirs), jnp.where(own, theirs, mine)], axis=0).astype(BF)
        x, y, z = net.at
        for p in range(3):
            for w, lo in where:
                hi = lo + G.shape[-1]
                G[(*w, z, y, x, p)] = both[p * 16:(p + 1) * 16, lo:hi]

    def bias_copy(d):
        return remote(bias.at[t], bias.at[t], psem.at[0, 3], psem.at[1, 3], net.along(2, d))

    for m in range(3):
        pre(m).start()
    pre(0).wait_recv()
    assemble(0, GA, [((net.core,), 0)], 0, 256)
    a.start(0, 0, 1)
    assemble(0, GB, [((net.core,), 0)], 512, 128)
    b.start(0, 2, 3)
    for m in (1, 2):
        pre(m).wait_recv()
        assemble(m, GC, [((j, net.core, m - 1), 128 * j) for j in range(3)], 0, 384)
    c.start(0, 4, 5)
    for d in (1, 2, 3):
        bias_copy(d).start()
    a.wait(9, 1)
    a.start(1, 6, 7)
    b.wait(9, 3)
    b.start(1, 8, 9)
    c.wait(9, 5)
    c.start(1, 10, 11)
    a.wait(36, 7)
    for d, r in zip(NEAR_FIRST, (13, 14, 15)):
        a.start(2, 12, r, (d,))
    for p in range(3):
        a.slab(p, 0, 16, 17).start()
    b.wait(36, 9)
    b.start(2, 18, 19)
    c.wait(36, 11)
    for j in range(3):
        third(j).start(2, 22 + 6 * j, 23 + 6 * j, (1, 3))
    for d, r in zip(NEAR_FIRST, (13, 14, 15)):
        a.wait(48, r)
        for p in range(3):
            a.slab(p, d, 16, 17).start()
    a.wait(192, 17)
    remote(bias.at[pl.ds(0, 3)], bias.at[pl.ds(0, 3)], psem.at[0, 3], psem.at[1, 3], net.sibling()).wait()

    def w_a(z):
        return jnp.concatenate([GA[core, z].reshape(D, 256) for core in range(2)], axis=1)

    def w_b(z):
        return jnp.concatenate([GB[core, z].reshape(D, 128) for core in range(2)], axis=1)

    def pair(m, z, j):
        return jnp.concatenate([GC[j, core, m, z].reshape(D, 128) for core in range(2)], axis=1)

    x = fin[...]
    for z in range(NZ):
        qkv[z, :, 0:512] = (mm(x, w_a(z)) + bias[z, :, 0:512]).astype(BF)
    b.wait(144, 19)
    b.whole(20, 21).start()
    b.wait(192, 21)
    last = mm(fin[...], jnp.concatenate([w_b(z)[:, :HD] for z in range(NZ)], axis=1))
    for z in range(NZ):
        qkv[z, :, 512:576] = (last[:, z * 64:(z + 1) * 64] + bias[z, :, 512:576]).astype(BF)

    def attend(z):
        for i in range(images):
            rs = pl.ds(i * SEQ, SEQ)
            blk = qkv[z, rs, :]
            alive = lax.broadcasted_iota(jnp.int32, (SEQ - TAIL, 1), 0) + TAIL < PATCHES + lens[t * images + i]
            outs = []
            for h in range(HZ):
                q = (blk[:, h * HD:(h + 1) * HD] * 0.125).astype(BF)
                k = blk[:, QW + h * HD:QW + (h + 1) * HD]
                v = blk[:, 2 * QW + h * HD:2 * QW + (h + 1) * HD]
                s = mm(k, q, NT)
                s = jnp.concatenate([s[:TAIL], jnp.where(alive, s[TAIL:], MASKED)], axis=0)
                e = jnp.exp(s - jnp.max(s, axis=0, keepdims=True))
                p = (e * (1.0 / jnp.sum(e, axis=0, keepdims=True))).astype(BF)
                probs[z, i * HZ + h] = p
                outs.append(mm(p, v, TN).astype(BF))
            att[z, rs, :] = jnp.concatenate(outs, axis=1)

    def onward(j):
        third(j).wait(96, 23 + 6 * j)
        third(j).pass_along(24 + 6 * j, 25 + 6 * j)

    def relay(j):
        third(j).wait(48, 25 + 6 * j)
        third(j).whole(26 + 6 * j, 27 + 6 * j).start()

    onward(0)
    attend(0)
    attend(1)
    onward(1)
    attend(2)
    attend(3)
    onward(2)
    relay(0)

    for load_ in loads[12:]:
        load_.wait()
    wout = jnp.concatenate([w_b(z)[:, HD:] for z in range(NZ)], axis=1)
    for i in range(images):
        rs = pl.ds(i * SEQ, SEQ)
        h = inp[rs, :] + mm(jnp.concatenate([att[z, rs, :] for z in range(NZ)], axis=1), wout, NT) + row(ob_)
        mid[rs, :] = h
        sin[rs, :] = (stats(h)[0] * row(g2_) + row(b2_)).astype(BF)

    relay(1)

    @pl.loop(0, 3)
    def _(j):
        third(j).wait(192, 27 + 6 * j)
        for z in range(NZ):
            ub = jnp.concatenate([bias[z, :, pl.ds(pl.multiple_of(o + j * 128, 128), 128)] for o in (640, 1024)], axis=1)
            u = mm(sin[...], pair(0, z, j)) + ub
            dh = mm(cot[...], pair(1, z, j))
            g, slope = gelu_pair(u)
            here = pl.ds(pl.multiple_of((j * NZ + z) * 256, 256), 256)
            hid[:, here] = g.astype(BF)
            dup[:, here] = (dh * slope).astype(BF)

        @pl.when(j == 0)
        def _():
            relay(2)

    total = None
    for j in range(3):
        w = jnp.concatenate([pair(0, z, j) for z in range(NZ)], axis=1)
        piece = mm(dup[:, j * 1024:(j + 1) * 1024], w, NT)
        total = piece if total is None else total + piece
    dmid[...] = total
    for i in range(images):
        rs = pl.ds(i * SEQ, SEQ)
        n, r = stats(mid[rs, :])
        d = cot[rs, :].astype(F32) + norm_back(dmid[rs, :], n, r, row(g2_))
        dmid[rs, :] = d
        dml[rs, :] = d.astype(BF)
    wout = jnp.concatenate([w_b(z)[:, HD:] for z in range(NZ)], axis=1)
    d = mm(dml[...], wout).astype(BF)
    for z in range(NZ):
        dat[z] = d[:, z * QW:(z + 1) * QW]

    def attend_back(z):
        for i in range(images):
            rs = pl.ds(i * SEQ, SEQ)
            blk = qkv[z, rs, :]
            dab = dat[z, rs, :]
            kt = blk[:, QW:2 * QW].T
            dq, dk, dv = [], [], []
            for h in range(HZ):
                q = blk[:, h * HD:(h + 1) * HD]
                v = blk[:, 2 * QW + h * HD:2 * QW + (h + 1) * HD]
                do = dab[:, h * HD:(h + 1) * HD]
                p = probs[z, i * HZ + h]
                dv.append(mm(p, do).astype(BF))
                pf = p.astype(F32)
                x = mm(v, do, NT) * pf
                ds = (x - pf * jnp.sum(x, axis=0, keepdims=True)).astype(BF)
                dk.append((mm(ds, q) * 0.125).astype(BF))
                dq.append(mm(kt[h * HD:(h + 1) * HD], ds))
            dq = (jnp.concatenate(dq, axis=0).T * 0.125).astype(BF)
            dqkv[z, rs, :] = jnp.concatenate([dq] + dk + dv, axis=1)

    @pl.loop(0, NZ // 2)
    def _(w):
        attend_back(2 * w)
        attend_back(2 * w + 1)

    def d_first(slices):
        w = jnp.concatenate([w for z in range(NZ) for w in (w_a(z), w_b(z)[:, :HD])], axis=1)
        x = jnp.concatenate([jnp.concatenate([dqkv[z, sl, :] for z in range(NZ)], axis=1) for sl in slices], axis=0)
        return mm(x, w, NT)

    tails = [pl.ds(i * SEQ + TAIL, SEQ - TAIL) for i in range(images)]
    n, r = stats(jnp.concatenate([inp[sl, :] for sl in tails], axis=0))
    d = jnp.concatenate([dmid[sl, :] for sl in tails], axis=0) + norm_back(d_first(tails), n, r, row(g1_))
    total = exact(jnp.concatenate(hots, axis=1), d)
    for i, sl in enumerate(tails):
        tgrad[sl, :] = jnp.where(lives[i], 0.0, d[i * (SEQ - TAIL):(i + 1) * (SEQ - TAIL)])
    part[...] = jnp.concatenate([total, jnp.zeros((128 - PROMPTS, D), F32)], axis=0)

    core, chip = net.core, net.chip
    mine = pl.ds(pl.multiple_of(core * 384, 128), 384)
    theirs = pl.ds(pl.multiple_of((1 - core) * 384, 128), 384)
    here = pl.ds(pl.multiple_of(chip * 8, 8), 8)

    def rest(i):
        lo = pl.ds(i * SEQ, TAIL)
        n, r = stats(inp[lo, :])
        tgrad[lo, :] = dmid[lo, :] + norm_back(d_first([lo]), n, r, row(g1_))

    def down():
        @pl.loop(0, images)
        def _(i):
            rs = pl.ds(pl.multiple_of(i * SEQ, 16), SEQ)
            acc = None
            for j in range(3):
                w = jnp.concatenate([pair(1, z, j) for z in range(NZ)], axis=1)
                piece = mm(hid[rs, j * 1024:(j + 1) * 1024], w, NT)
                acc = piece if acc is None else acc + piece
            out[rs, :] = (mid[rs, :] + acc + row(db_)).astype(BF)

    swap = remote(part.at[:, theirs], half, tsem.at[0], tsem.at[1], net.sibling())
    swap.start()
    rest(0)
    swap.wait()
    part[:, mine] = part[:, mine] + half[...]
    for i in range(1, 16):
        dst = lax.rem(chip + i, 16)
        remote(part.at[pl.ds(pl.multiple_of(dst * 8, 8), 8), mine], slots.at[i], tsem.at[2], tsem.at[3], net.plane(i)).start()
    rest(1)
    tout = pltpu.make_async_copy(tgrad, tgrad_h, osem.at[0])
    tout.start()
    down()
    oout = pltpu.make_async_copy(out, out_h, osem.at[1])
    oout.start()
    fifteen = slots.at[pl.ds(1, 15)]
    remote(fifteen, fifteen, tsem.at[2], tsem.at[3], net.sibling()).wait()
    acc = part[here, mine]
    for i in range(1, 16):
        acc = acc + slots[i]
    zslots[t] = acc
    for d in (1, 2, 3):
        remote(zslots.at[t], zslots.at[t], tsem.at[4], tsem.at[5], net.along(2, d)).start()
    three = zslots.at[pl.ds(0, 3)]
    remote(three, three, tsem.at[4], tsem.at[5], net.sibling()).wait()
    final[here, mine] = (zslots[0] + zslots[1]) + (zslots[2] + zslots[3])
    ref = final.at[here, mine]
    for i in range(1, 16):
        remote(ref, ref, tsem.at[6], tsem.at[7], net.plane(i)).start()
    for m in range(3):
        pre(m).wait_send()
    for part_, sems in ((a, (0, 6, 12, 16)), (b, (2, 8, 18, 20))):
        for blocks, sem in zip((9, 36, 144, 192), sems):
            part_.wait_sent(blocks, sem)
    c.wait_sent(9, 4)
    c.wait_sent(36, 10)
    for j in range(3):
        third(j).wait_sent(96, 22 + 6 * j)
        third(j).wait_sent(48, 24 + 6 * j)
        third(j).wait_sent(192, 26 + 6 * j)
    many = final.at[pl.ds(0, 120), mine]
    remote(many, many, tsem.at[6], tsem.at[7], net.sibling()).wait()
    done = remote(final.at[pl.ds(0, 104), mine], final.at[pl.ds(0, 104), mine], tsem.at[8], tsem.at[9], net.sibling())
    done.start()
    done.wait()
    pbuf[...] = final[0:PROMPTS, :]
    pout = pltpu.make_async_copy(pbuf, pgrad_h, osem.at[2])
    pout.start()
    pout.wait()
    tout.wait()
    oout.wait()


def hand_over(pairs, *refs):
    n = len(pairs)
    srcs, dsts, bufs, sem = refs[:n], refs[n:2 * n], refs[2 * n:3 * n], refs[3 * n]
    pieces = []
    for src, dst, buf, rows in zip(srcs, dsts, bufs, pairs):
        for first in range(0, src.shape[0], rows):
            pieces.append((src, dst, buf, pl.ds(first, min(rows, src.shape[0] - first))))
    into = [pltpu.make_async_copy(s.at[r], b.at[r], sem.at[0, k]) for k, (s, d, b, r) in enumerate(pieces)]
    away = [pltpu.make_async_copy(b.at[r], d.at[r], sem.at[1, k]) for k, (s, d, b, r) in enumerate(pieces)]
    for copy in into:
        copy.start()
    for first, second in zip(into, away):
        first.wait()
        second.start()
    for copy in away:
        copy.wait()


def body(tokens, prompt_table, lengths, table_rows, ln1_gain, ln1_bias, w_qkv, qv_bias, w_out, out_bias,
         ln2_gain, ln2_bias, w_up, up_bias, w_down, down_bias, cotangent):
    rows = tokens.shape[0]
    images = rows // SEQ
    any_ = pl.BlockSpec(memory_space=pl.ANY)
    args = (lengths, tokens, prompt_table, table_rows, ln1_gain, ln1_bias, out_bias, ln2_gain, ln2_bias, down_bias, cotangent,
            qv_bias, up_bias, w_qkv, w_out.T, w_up, w_down.T)
    vmem = lambda shape, dtype: pltpu.VMEM(shape, dtype)
    token_out, grad_out, table_out = pl.pallas_call(
        functools.partial(compute, rows),
        out_shape=(jax.ShapeDtypeStruct((rows, D), BF), jax.ShapeDtypeStruct((rows, D), F32), jax.ShapeDtypeStruct((PROMPTS, D), F32)),
        in_specs=[any_] * len(args),
        out_specs=(any_, any_, any_),
        scratch_shapes=[pltpu.SMEM(lengths.shape, lengths.dtype)] + [vmem(v.shape, v.dtype) for v in args[1:]] + [
            vmem((rows, D), F32),
            vmem((rows, D), BF),
            vmem((NZ, rows, 3 * QW), BF),
            vmem((NZ, images * HZ, SEQ, SEQ), BF),
            vmem((NZ, rows, QW), BF),
            vmem((rows, D), F32),
            vmem((rows, D), BF),
            vmem((rows, NZ * FZ), BF),
            vmem((rows, NZ * FZ), BF),
            vmem((rows, D), F32),
            vmem((rows, D), BF),
            vmem((NZ, rows, QW), BF),
            vmem((NZ, rows, 3 * QW), BF),
            vmem((rows, D), BF),
            vmem((rows, D), F32),
            vmem((2, 4, 4, 4, 3, 16, 256), BF),
            vmem((2, 4, 4, 4, 3, 16, 128), BF),
            vmem((3, 2, 2, 4, 4, 4, 3, 16, 128), BF),
            vmem((3, 24, 768), F32),
            vmem((3, 24, 768), F32),
            vmem((NZ, 1, 1408), F32),
            vmem((128, D), F32),
            vmem((128, 384), F32),
            vmem((16, 8, 384), F32),
            vmem((NZ, 8, 384), F32),
            vmem((128, D), F32),
            vmem((PROMPTS, D), F32),
            DMA((len(args),)), DMA((2, 4)), DMA((40,)), DMA((10,)), DMA((3,)),
        ],
        compiler_params=pltpu.CompilerParams(collective_id=1, has_side_effects=True, vmem_limit_bytes=63 * 2**20),
    )(*args)
    outs = (token_out, grad_out, table_out)
    return pl.pallas_call(
        functools.partial(hand_over, (304, 152, PROMPTS)),
        out_shape=tuple(jax.ShapeDtypeStruct(v.shape, v.dtype) for v in outs),
        in_specs=[any_] * 3,
        out_specs=(any_, any_, any_),
        scratch_shapes=[vmem(v.shape, v.dtype) for v in outs] + [DMA((2, 7))],
    )(*outs)


def solution(mesh):
    row = P(("dp", "tensor"), None)
    return jax.shard_map(
        body, mesh=mesh,
        in_specs=(row, P(), P("dp"), P("dp", None), P(), P(), P(None, "dp", "tensor"), P(None, "tensor"), P("tensor", "dp"),
                  P(), P(), P(), P("dp", "tensor"), P("tensor"), P("tensor", "dp"), P(), row),
        out_specs=(row, row, P()), check_vma=False)
```

```python
import functools

import jax
import jax.numpy as jnp
from jax import lax
from jax.experimental import pallas as pl
from jax.experimental.pallas import tpu as pltpu
from jax.sharding import PartitionSpec as P

D = 768
HD = 64
PATCHES = 197
PROMPTS = 100
SEQ = 304
NZ = 4
HZ = 3
QW = 192
FZ = 768
EPSILON = 1e-06
MASKED = -1e30
F32 = jnp.float32
BF = jnp.bfloat16
NN = (((1,), (0,)), ((), ()))
NT = (((1,), (1,)), ((), ()))
TN = (((0,), (0,)), ((), ()))
MESH = pl.DeviceIdType.MESH
DMA = pltpu.SemaphoreType.DMA
ORDERS = ((0, 1, 2), (1, 2, 0), (2, 0, 1))
NEAR_FIRST = (1, 3, 2)
TAIL = 192


def mm(a, b, dims=NN):
    return lax.dot_general(a, b, dims, preferred_element_type=F32)


def exact(a, b, dims=NN):
    return lax.dot_general(a, b, dims, precision=lax.Precision.HIGHEST, preferred_element_type=F32)


def gelu_pair(u):
    t = 1.0 / (1.0 + (0.3275911 * 0.7071067811865476) * jnp.abs(u))
    e = jnp.exp(-0.5 * (u * u))
    poly = t * (0.254829592 + t * (-0.284496736 + t * (1.421413741 + t * (-1.453152027 + t * 1.061405429))))
    half = 0.5 * poly * e
    cdf = jnp.where(u >= 0, 1.0 - half, half)
    return u * cdf, cdf + u * (0.3989422804014327 * e)


def stats(h):
    c = h - jnp.mean(h, axis=-1, keepdims=True)
    r = lax.rsqrt(jnp.mean(c * c, axis=-1, keepdims=True) + EPSILON)
    return c * r, r


def norm_back(g, n, r, gain):
    e = g * gain
    return r * (e - jnp.mean(e, axis=-1, keepdims=True) - n * jnp.mean(e * n, axis=-1, keepdims=True))


class Net:
    def __init__(self):
        dp = lax.axis_index("dp")
        self.core = lax.rem(dp, 2)
        self.chip = lax.div(dp, 2)
        self.at = (lax.rem(self.chip, 4), lax.div(self.chip, 4), lax.axis_index("tensor"))

    def device(self, at, core):
        return ((at[1] * 4 + at[0]) * 2 + core, at[2])

    def moved(self, axis, step):
        at = list(self.at)
        at[axis] = lax.rem(at[axis] + step, 4)
        return tuple(at)

    def sibling(self):
        return self.device(self.at, 1 - self.core)

    def along(self, axis, step):
        return self.device(self.moved(axis, step), self.core)

    def plane(self, i):
        return (lax.rem(self.chip + i, 16) * 2 + self.core, self.at[2])

    def greet(self):
        sem = pltpu.get_barrier_semaphore()
        peers = [self.sibling()] + [self.plane(i) for i in range(1, 16)] + [self.along(2, d) for d in (1, 2, 3)]
        for peer in peers:
            pl.semaphore_signal(sem, inc=1, device_id=peer, device_id_type=MESH)
        return len(peers)


def remote(src, dst, send, recv, to):
    return pltpu.make_async_remote_copy(src_ref=src, dst_ref=dst, send_sem=send, recv_sem=recv, device_id=to, device_id_type=MESH)


class Part:
    def __init__(self, net, G, where, sems):
        self.net, self.G, self.where, self.sems = net, G, where, sems

    def view(self, p, phase, at, half=None):
        at = list(at)
        for axis in ORDERS[p][:phase]:
            at[axis] = slice(None)
        if half is not None:
            at[ORDERS[p][0]] = pl.ds(2 * half, 2)
        return self.G.at[(*self.where, at[2], at[1], at[0], p)]

    def start(self, phase, send, recv, ds=NEAR_FIRST):
        for d in ds:
            for p in range(3):
                ref = self.view(p, phase, self.net.at)
                remote(ref, ref, self.sems.at[send], self.sems.at[recv], self.net.along(ORDERS[p][phase], d)).start()

    def pass_along(self, send, recv):
        for p in range(3):
            for d in (1, 3):
                axis = ORDERS[p][2]
                ref = self.view(p, 2, self.net.moved(axis, 4 - d), d // 2)
                remote(ref, ref, self.sems.at[send], self.sems.at[recv], self.net.along(axis, d)).start()

    def bulk(self, blocks):
        all_ = slice(None)
        piece = {9: (0, 0, pl.ds(0, 3)), 36: (0, all_, pl.ds(0, 3)), 48: (0,), 96: (pl.ds(0, 2),), 144: (all_, all_, pl.ds(0, 3)), 192: ()}[blocks]
        return self.G.at[(*self.where, *piece)]

    def wait(self, blocks, sem):
        ref = self.bulk(blocks)
        remote(ref, ref, self.sems.at[sem], self.sems.at[sem], self.net.sibling()).wait_recv()

    def wait_sent(self, blocks, sem):
        ref = self.bulk(blocks)
        remote(ref, ref, self.sems.at[sem], self.sems.at[sem], self.net.sibling()).wait_send()

    def slab(self, p, d, send, recv):
        ref = self.view(p, 2, self.net.moved(ORDERS[p][2], 4 - d) if d else self.net.at)
        return remote(ref, ref, self.sems.at[send], self.sems.at[recv], self.net.sibling())

    def whole(self, send, recv):
        ref = self.bulk(192)
        return remote(ref, ref, self.sems.at[send], self.sems.at[recv], self.net.sibling())


def compute(rows, lens_h, tok_h, table_h, trows_h, g1_h, b1_h, ob_h, g2_h, b2_h, db_h, cot_h, qvb_h, upb_h, wq_h, wo_h, wu_h, wd_h,
            out_h, tgrad_h, pgrad_h,
            lens, tok, table, trows, g1_, b1_, ob_, g2_, b2_, db_, cot, qvb, upb, wq, wo, wu, wd,
            inp, fin, qkv, probs, dscores, att, mid, sin, hid, dup, dmid, dml, dat, dqkv, out, tgrad,
            GA, GB, GC, stage, other, bias, part, half, slots, zslots, final, pbuf, isem, psem, gsem, tsem, osem):
    images = rows // SEQ
    net = Net()
    t = net.at[2]
    n_peers = net.greet()

    loads = []
    for k, (src, dst) in enumerate(((wq_h, wq), (wo_h, wo), (wu_h, wu), (wd_h, wd), (lens_h, lens), (trows_h, trows), (table_h, table),
                                    (tok_h, tok), (qvb_h, qvb), (upb_h, upb), (g1_h, g1_), (b1_h, b1_), (ob_h, ob_), (g2_h, g2_),
                                    (b2_h, b2_), (db_h, db_), (cot_h, cot))):
        loads.append(pltpu.make_async_copy(src, dst, isem.at[k]))
    for load in loads:
        load.start()
    for load in loads[:4]:
        load.wait()
    stage[0] = jnp.concatenate([wq[0], wq[1], wq[2], wo[...]], axis=1)
    stage[1] = wu[...]
    stage[2] = wd[...]
    for load in loads[4:12]:
        load.wait()

    hots, lives = [], []
    for i in range(images):
        length = lens[t * images + i]
        base = jnp.concatenate([trows[pl.ds(t * images + i, 1), :], jnp.full((1, 384 - PROMPTS), -1, jnp.int32)], axis=1)
        slot = pltpu.roll(base, PATCHES - TAIL, 1)[:, :SEQ - TAIL]
        place = lax.broadcasted_iota(jnp.int32, (1, SEQ - TAIL), 1) + TAIL
        slot = jnp.where((place >= PATCHES) & (place < PATCHES + length), slot, -1)
        hots.append((lax.broadcasted_iota(jnp.int32, (PROMPTS, SEQ - TAIL), 0) == slot).astype(F32))
        place = lax.broadcasted_iota(jnp.int32, (SEQ - TAIL, 1), 0) + TAIL
        lives.append((place >= PATCHES) & (place < PATCHES + length))
    row = lambda ref: ref[...].reshape(1, D)
    for i in range(images):
        lo, hi = pl.ds(i * SEQ, TAIL), pl.ds(i * SEQ + TAIL, SEQ - TAIL)
        inp[lo, :] = tok[lo, :].astype(F32)
        inp[hi, :] = jnp.where(lives[i], exact(hots[i], table[...], TN), tok[hi, :].astype(F32))
        rs = pl.ds(i * SEQ, SEQ)
        fin[rs, :] = (stats(inp[rs, :])[0] * row(g1_) + row(b1_)).astype(BF)
    bias[t] = jnp.concatenate([qvb[0:1, :], jnp.zeros((1, QW), F32), qvb[1:2, :], jnp.zeros((1, 64), F32), upb[...].reshape(1, FZ)], axis=1)

    a = Part(net, GA, (net.core,), gsem)
    b = Part(net, GB, (net.core,), gsem)
    c = Part(net, GC, (slice(None), net.core, slice(None)), gsem)

    def third(j):
        return Part(net, GC, (j, net.core, slice(None)), gsem)

    pl.semaphore_wait(pltpu.get_barrier_semaphore(), n_peers)

    def pre(m):
        return remote(stage.at[m], other.at[m], psem.at[0, m], psem.at[1, m], net.sibling())

    def assemble(m, G, where, first, width):
        cs = pl.ds(pl.multiple_of(first + net.core * width, 128), width)
        mine, theirs = stage[m, :, cs], other[m, :, cs]
        own = net.core == 0
        both = jnp.concatenate([jnp.where(own, mine, theirs), jnp.where(own, theirs, mine)], axis=0).astype(BF)
        x, y, z = net.at
        for p in range(3):
            for w, lo in where:
                hi = lo + G.shape[-1]
                G[(*w, z, y, x, p)] = both[p * 16:(p + 1) * 16, lo:hi]

    def bias_copy(d):
        return remote(bias.at[t], bias.at[t], psem.at[0, 3], psem.at[1, 3], net.along(2, d))

    for m in range(3):
        pre(m).start()
    pre(0).wait_recv()
    assemble(0, GA, [((net.core,), 0)], 0, 256)
    a.start(0, 0, 1)
    assemble(0, GB, [((net.core,), 0)], 512, 128)
    b.start(0, 2, 3)
    for m in (1, 2):
        pre(m).wait_recv()
        assemble(m, GC, [((j, net.core, m - 1), 128 * j) for j in range(3)], 0, 384)
    c.start(0, 4, 5)
    for d in (1, 2, 3):
        bias_copy(d).start()
    a.wait(9, 1)
    a.start(1, 6, 7)
    b.wait(9, 3)
    b.start(1, 8, 9)
    c.wait(9, 5)
    c.start(1, 10, 11)
    a.wait(36, 7)
    for d, r in zip(NEAR_FIRST, (13, 14, 15)):
        a.start(2, 12, r, (d,))
    for p in range(3):
        a.slab(p, 0, 16, 17).start()
    b.wait(36, 9)
    b.start(2, 18, 19)
    c.wait(36, 11)
    for j in range(3):
        third(j).start(2, 22 + 6 * j, 23 + 6 * j, (1, 3))
    for d, r in zip(NEAR_FIRST, (13, 14, 15)):
        a.wait(48, r)
        for p in range(3):
            a.slab(p, d, 16, 17).start()
    a.wait(192, 17)
    remote(bias.at[pl.ds(0, 3)], bias.at[pl.ds(0, 3)], psem.at[0, 3], psem.at[1, 3], net.sibling()).wait()

    def w_a(z):
        return jnp.concatenate([GA[core, z].reshape(D, 256) for core in range(2)], axis=1)

    def w_b(z):
        return jnp.concatenate([GB[core, z].reshape(D, 128) for core in range(2)], axis=1)

    def pair(m, z, j):
        return jnp.concatenate([GC[j, core, m, z].reshape(D, 128) for core in range(2)], axis=1)

    x = fin[...]
    for z in range(NZ):
        qkv[z, :, 0:512] = (mm(x, w_a(z)) + bias[z, :, 0:512]).astype(BF)
    b.wait(144, 19)
    b.whole(20, 21).start()
    b.wait(192, 21)
    last = mm(fin[...], jnp.concatenate([w_b(z)[:, :HD] for z in range(NZ)], axis=1))
    for z in range(NZ):
        qkv[z, :, 512:576] = (last[:, z * 64:(z + 1) * 64] + bias[z, :, 512:576]).astype(BF)

    def attend(z):
        for i in range(images):
            rs = pl.ds(i * SEQ, SEQ)
            blk = qkv[z, rs, :]
            alive = lax.broadcasted_iota(jnp.int32, (SEQ - TAIL, 1), 0) + TAIL < PATCHES + lens[t * images + i]
            outs = []
            for h in range(HZ):
                q = (blk[:, h * HD:(h + 1) * HD] * 0.125).astype(BF)
                k = blk[:, QW + h * HD:QW + (h + 1) * HD]
                v = blk[:, 2 * QW + h * HD:2 * QW + (h + 1) * HD]
                s = mm(k, q, NT)
                s = jnp.concatenate([s[:TAIL], jnp.where(alive, s[TAIL:], MASKED)], axis=0)
                e = jnp.exp(s - jnp.max(s, axis=0, keepdims=True))
                p = (e * (1.0 / jnp.sum(e, axis=0, keepdims=True))).astype(BF)
                probs[z, i * HZ + h] = p
                outs.append(mm(p, v, TN).astype(BF))
            att[z, rs, :] = jnp.concatenate(outs, axis=1)

    def onward(j):
        third(j).wait(96, 23 + 6 * j)
        third(j).pass_along(24 + 6 * j, 25 + 6 * j)

    def relay(j):
        third(j).wait(48, 25 + 6 * j)
        third(j).whole(26 + 6 * j, 27 + 6 * j).start()

    onward(0)
    attend(0)
    attend(1)
    onward(1)
    attend(2)
    attend(3)
    onward(2)
    relay(0)

    for load_ in loads[12:]:
        load_.wait()
    wout = jnp.concatenate([w_b(z)[:, HD:] for z in range(NZ)], axis=1)
    for i in range(images):
        rs = pl.ds(i * SEQ, SEQ)
        h = inp[rs, :] + mm(jnp.concatenate([att[z, rs, :] for z in range(NZ)], axis=1), wout, NT) + row(ob_)
        mid[rs, :] = h
        sin[rs, :] = (stats(h)[0] * row(g2_) + row(b2_)).astype(BF)

    relay(1)

    @pl.loop(0, 3)
    def _(j):
        third(j).wait(192, 27 + 6 * j)
        for z in range(NZ):
            ub = jnp.concatenate([bias[z, :, pl.ds(pl.multiple_of(o + j * 128, 128), 128)] for o in (640, 1024)], axis=1)
            u = mm(sin[...], pair(0, z, j)) + ub
            dh = mm(cot[...], pair(1, z, j))
            g, slope = gelu_pair(u)
            here = pl.ds(pl.multiple_of((j * NZ + z) * 256, 256), 256)
            hid[:, here] = g.astype(BF)
            dup[:, here] = (dh * slope).astype(BF)

        @pl.when(j == 0)
        def _():
            relay(2)

    total = None
    for j in range(3):
        w = jnp.concatenate([pair(0, z, j) for z in range(NZ)], axis=1)
        piece = mm(dup[:, j * 1024:(j + 1) * 1024], w, NT)
        total = piece if total is None else total + piece
    dmid[...] = total
    for i in range(images):
        rs = pl.ds(i * SEQ, SEQ)
        n, r = stats(mid[rs, :])
        d = cot[rs, :].astype(F32) + norm_back(dmid[rs, :], n, r, row(g2_))
        dmid[rs, :] = d
        dml[rs, :] = d.astype(BF)
    wout = jnp.concatenate([w_b(z)[:, HD:] for z in range(NZ)], axis=1)
    d = mm(dml[...], wout).astype(BF)
    for z in range(NZ):
        dat[z] = d[:, z * QW:(z + 1) * QW]

    def attend_back(z):
        for i in range(images):
            rs, hi = pl.ds(i * SEQ, SEQ), pl.ds(i * SEQ + TAIL, SEQ - TAIL)
            blk = qkv[z, rs, :]
            dab = dat[z, rs, :]
            kt = blk[:, QW:2 * QW].T
            dq, dk, dv = [], [], []
            for h in range(HZ):
                v = blk[:, 2 * QW + h * HD:2 * QW + (h + 1) * HD]
                do = dab[:, h * HD:(h + 1) * HD]
                p = probs[z, i * HZ + h]
                dv.append(mm(p[TAIL:], do).astype(BF))
                pf = p.astype(F32)
                x = mm(v, do, NT) * pf
                ds = (x - pf * jnp.sum(x, axis=0, keepdims=True)).astype(BF)
                dscores[z, i * HZ + h] = ds
                dk.append((mm(ds[TAIL:], blk[:, h * HD:(h + 1) * HD]) * 0.125).astype(BF))
                dq.append(mm(kt[h * HD:(h + 1) * HD], ds[:, 128:]))
            dq = (jnp.concatenate(dq, axis=0).T[TAIL - 128:] * 0.125).astype(BF)
            dqkv[z, hi, :] = jnp.concatenate([dq] + dk + dv, axis=1)

    def attend_back_rest(z):
        for i in range(images):
            rs, lo = pl.ds(i * SEQ, SEQ), pl.ds(i * SEQ, TAIL)
            blk = qkv[z, rs, :]
            dab = dat[z, rs, :]
            kt = blk[:, QW:2 * QW].T
            dq, dk, dv = [], [], []
            for h in range(HZ):
                dv.append(mm(probs[z, i * HZ + h, :TAIL, :], dab[:, h * HD:(h + 1) * HD]).astype(BF))
                ds = dscores[z, i * HZ + h]
                dk.append((mm(ds[:TAIL], blk[:, h * HD:(h + 1) * HD]) * 0.125).astype(BF))
                dq.append(mm(kt[h * HD:(h + 1) * HD], ds[:, :256]))
            dq = (jnp.concatenate(dq, axis=0).T[:TAIL] * 0.125).astype(BF)
            dqkv[z, lo, :] = jnp.concatenate([dq] + dk + dv, axis=1)

    @pl.loop(0, NZ // 2)
    def _(w):
        attend_back(2 * w)
        attend_back(2 * w + 1)

    def d_first(slices):
        w = jnp.concatenate([w for z in range(NZ) for w in (w_a(z), w_b(z)[:, :HD])], axis=1)
        x = jnp.concatenate([jnp.concatenate([dqkv[z, sl, :] for z in range(NZ)], axis=1) for sl in slices], axis=0)
        return mm(x, w, NT)

    tails = [pl.ds(i * SEQ + TAIL, SEQ - TAIL) for i in range(images)]
    n, r = stats(jnp.concatenate([inp[sl, :] for sl in tails], axis=0))
    d = jnp.concatenate([dmid[sl, :] for sl in tails], axis=0) + norm_back(d_first(tails), n, r, row(g1_))
    total = exact(jnp.concatenate(hots, axis=1), d)
    for i, sl in enumerate(tails):
        tgrad[sl, :] = jnp.where(lives[i], 0.0, d[i * (SEQ - TAIL):(i + 1) * (SEQ - TAIL)])
    part[...] = jnp.concatenate([total, jnp.zeros((128 - PROMPTS, D), F32)], axis=0)

    core, chip = net.core, net.chip
    mine = pl.ds(pl.multiple_of(core * 384, 128), 384)
    theirs = pl.ds(pl.multiple_of((1 - core) * 384, 128), 384)
    here = pl.ds(pl.multiple_of(chip * 8, 8), 8)

    def rest(i):
        lo = pl.ds(i * SEQ, TAIL)
        n, r = stats(inp[lo, :])
        tgrad[lo, :] = dmid[lo, :] + norm_back(d_first([lo]), n, r, row(g1_))

    def down():
        @pl.loop(0, images)
        def _(i):
            rs = pl.ds(pl.multiple_of(i * SEQ, 16), SEQ)
            acc = None
            for j in range(3):
                w = jnp.concatenate([pair(1, z, j) for z in range(NZ)], axis=1)
                piece = mm(hid[rs, j * 1024:(j + 1) * 1024], w, NT)
                acc = piece if acc is None else acc + piece
            out[rs, :] = (mid[rs, :] + acc + row(db_)).astype(BF)

    swap = remote(part.at[:, theirs], half, tsem.at[0], tsem.at[1], net.sibling())
    swap.start()
    swap.wait()
    part[:, mine] = part[:, mine] + half[...]
    for i in range(1, 16):
        dst = lax.rem(chip + i, 16)
        remote(part.at[pl.ds(pl.multiple_of(dst * 8, 8), 8), mine], slots.at[i], tsem.at[2], tsem.at[3], net.plane(i)).start()

    @pl.loop(0, NZ // 2)
    def _(w):
        attend_back_rest(2 * w)
        attend_back_rest(2 * w + 1)

    fifteen = slots.at[pl.ds(1, 15)]
    remote(fifteen, fifteen, tsem.at[2], tsem.at[3], net.sibling()).wait()
    acc = part[here, mine]
    for i in range(1, 16):
        acc = acc + slots[i]
    zslots[t] = acc
    for d in (1, 2, 3):
        remote(zslots.at[t], zslots.at[t], tsem.at[4], tsem.at[5], net.along(2, d)).start()
    rest(0)
    rest(1)
    tout = pltpu.make_async_copy(tgrad, tgrad_h, osem.at[0])
    tout.start()
    three = zslots.at[pl.ds(0, 3)]
    remote(three, three, tsem.at[4], tsem.at[5], net.sibling()).wait()
    final[here, mine] = (zslots[0] + zslots[1]) + (zslots[2] + zslots[3])
    ref = final.at[here, mine]
    for i in range(1, 16):
        remote(ref, ref, tsem.at[6], tsem.at[7], net.plane(i)).start()
    down()
    oout = pltpu.make_async_copy(out, out_h, osem.at[1])
    oout.start()
    for m in range(3):
        pre(m).wait_send()
    for part_, sems in ((a, (0, 6, 12, 16)), (b, (2, 8, 18, 20))):
        for blocks, sem in zip((9, 36, 144, 192), sems):
            part_.wait_sent(blocks, sem)
    c.wait_sent(9, 4)
    c.wait_sent(36, 10)
    for j in range(3):
        third(j).wait_sent(96, 22 + 6 * j)
        third(j).wait_sent(48, 24 + 6 * j)
        third(j).wait_sent(192, 26 + 6 * j)
    many = final.at[pl.ds(0, 120), mine]
    remote(many, many, tsem.at[6], tsem.at[7], net.sibling()).wait()
    done = remote(final.at[pl.ds(0, 104), mine], final.at[pl.ds(0, 104), mine], tsem.at[8], tsem.at[9], net.sibling())
    done.start()
    done.wait()
    pbuf[...] = final[0:PROMPTS, :]
    pout = pltpu.make_async_copy(pbuf, pgrad_h, osem.at[2])
    pout.start()
    pout.wait()
    tout.wait()
    oout.wait()


def hand_over(pairs, *refs):
    n = len(pairs)
    srcs, dsts, bufs, sem = refs[:n], refs[n:2 * n], refs[2 * n:3 * n], refs[3 * n]
    pieces = []
    for src, dst, buf, rows in zip(srcs, dsts, bufs, pairs):
        for first in range(0, src.shape[0], rows):
            pieces.append((src, dst, buf, pl.ds(first, min(rows, src.shape[0] - first))))
    into = [pltpu.make_async_copy(s.at[r], b.at[r], sem.at[0, k]) for k, (s, d, b, r) in enumerate(pieces)]
    away = [pltpu.make_async_copy(b.at[r], d.at[r], sem.at[1, k]) for k, (s, d, b, r) in enumerate(pieces)]
    for copy in into:
        copy.start()
    for first, second in zip(into, away):
        first.wait()
        second.start()
    for copy in away:
        copy.wait()


def body(tokens, prompt_table, lengths, table_rows, ln1_gain, ln1_bias, w_qkv, qv_bias, w_out, out_bias,
         ln2_gain, ln2_bias, w_up, up_bias, w_down, down_bias, cotangent):
    rows = tokens.shape[0]
    images = rows // SEQ
    any_ = pl.BlockSpec(memory_space=pl.ANY)
    args = (lengths, tokens, prompt_table, table_rows, ln1_gain, ln1_bias, out_bias, ln2_gain, ln2_bias, down_bias, cotangent,
            qv_bias, up_bias, w_qkv, w_out.T, w_up, w_down.T)
    vmem = lambda shape, dtype: pltpu.VMEM(shape, dtype)
    token_out, grad_out, table_out = pl.pallas_call(
        functools.partial(compute, rows),
        out_shape=(jax.ShapeDtypeStruct((rows, D), BF), jax.ShapeDtypeStruct((rows, D), F32), jax.ShapeDtypeStruct((PROMPTS, D), F32)),
        in_specs=[any_] * len(args),
        out_specs=(any_, any_, any_),
        scratch_shapes=[pltpu.SMEM(lengths.shape, lengths.dtype)] + [vmem(v.shape, v.dtype) for v in args[1:]] + [
            vmem((rows, D), F32),
            vmem((rows, D), BF),
            vmem((NZ, rows, 3 * QW), BF),
            vmem((NZ, images * HZ, SEQ, SEQ), BF),
            vmem((NZ, images * HZ, SEQ, SEQ), BF),
            vmem((NZ, rows, QW), BF),
            vmem((rows, D), F32),
            vmem((rows, D), BF),
            vmem((rows, NZ * FZ), BF),
            vmem((rows, NZ * FZ), BF),
            vmem((rows, D), F32),
            vmem((rows, D), BF),
            vmem((NZ, rows, QW), BF),
            vmem((NZ, rows, 3 * QW), BF),
            vmem((rows, D), BF),
            vmem((rows, D), F32),
            vmem((2, 4, 4, 4, 3, 16, 256), BF),
            vmem((2, 4, 4, 4, 3, 16, 128), BF),
            vmem((3, 2, 2, 4, 4, 4, 3, 16, 128), BF),
            vmem((3, 24, 768), F32),
            vmem((3, 24, 768), F32),
            vmem((NZ, 1, 1408), F32),
            vmem((128, D), F32),
            vmem((128, 384), F32),
            vmem((16, 8, 384), F32),
            vmem((NZ, 8, 384), F32),
            vmem((128, D), F32),
            vmem((PROMPTS, D), F32),
            DMA((len(args),)), DMA((2, 4)), DMA((40,)), DMA((10,)), DMA((3,)),
        ],
        compiler_params=pltpu.CompilerParams(collective_id=1, has_side_effects=True, vmem_limit_bytes=63 * 2**20),
    )(*args)
    outs = (token_out, grad_out, table_out)
    return pl.pallas_call(
        functools.partial(hand_over, (304, 152, PROMPTS)),
        out_shape=tuple(jax.ShapeDtypeStruct(v.shape, v.dtype) for v in outs),
        in_specs=[any_] * 3,
        out_specs=(any_, any_, any_),
        scratch_shapes=[vmem(v.shape, v.dtype) for v in outs] + [DMA((2, 7))],
    )(*outs)


def solution(mesh):
    row = P(("dp", "tensor"), None)
    return jax.shard_map(
        body, mesh=mesh,
        in_specs=(row, P(), P("dp"), P("dp", None), P(), P(), P(None, "dp", "tensor"), P(None, "tensor"), P("tensor", "dp"),
                  P(), P(), P(), P("dp", "tensor"), P("tensor"), P("tensor", "dp"), P(), row),
        out_specs=(row, row, P()), check_vma=False)
```

```python
import functools

import jax
import jax.numpy as jnp
from jax import lax
from jax.experimental import pallas as pl
from jax.experimental.pallas import tpu as pltpu
from jax.sharding import PartitionSpec as P

D = 768
HD = 64
PATCHES = 197
PROMPTS = 100
SEQ = 304
NZ = 4
HZ = 3
QW = 192
FZ = 768
EPSILON = 1e-06
MASKED = -1e30
F32 = jnp.float32
BF = jnp.bfloat16
NN = (((1,), (0,)), ((), ()))
NT = (((1,), (1,)), ((), ()))
TN = (((0,), (0,)), ((), ()))
MESH = pl.DeviceIdType.MESH
DMA = pltpu.SemaphoreType.DMA
ORDERS = ((0, 1, 2), (1, 2, 0), (2, 0, 1))
NEAR_FIRST = (1, 3, 2)
FAR_FIRST = (2, 1, 3)
PLANE = (10, 6, 9, 11, 14, 2, 8, 5, 7, 13, 15, 1, 3, 4, 12)
TAIL = 192


def mm(a, b, dims=NN):
    return lax.dot_general(a, b, dims, preferred_element_type=F32)


def exact(a, b, dims=NN):
    return lax.dot_general(a, b, dims, precision=lax.Precision.HIGHEST, preferred_element_type=F32)


def gelu_pair(u):
    t = 1.0 / (1.0 + (0.3275911 * 0.7071067811865476) * jnp.abs(u))
    e = jnp.exp(-0.5 * (u * u))
    poly = t * (0.254829592 + t * (-0.284496736 + t * (1.421413741 + t * (-1.453152027 + t * 1.061405429))))
    half = 0.5 * poly * e
    cdf = jnp.where(u >= 0, 1.0 - half, half)
    return u * cdf, cdf + u * (0.3989422804014327 * e)


def stats(h):
    c = h - jnp.mean(h, axis=-1, keepdims=True)
    r = lax.rsqrt(jnp.mean(c * c, axis=-1, keepdims=True) + EPSILON)
    return c * r, r


def norm_back(g, n, r, gain):
    e = g * gain
    return r * (e - jnp.mean(e, axis=-1, keepdims=True) - n * jnp.mean(e * n, axis=-1, keepdims=True))


class Net:
    def __init__(self):
        dp = lax.axis_index("dp")
        self.core = lax.rem(dp, 2)
        self.chip = lax.div(dp, 2)
        self.at = (lax.rem(self.chip, 4), lax.div(self.chip, 4), lax.axis_index("tensor"))

    def device(self, at, core):
        return ((at[1] * 4 + at[0]) * 2 + core, at[2])

    def moved(self, axis, step):
        at = list(self.at)
        at[axis] = lax.rem(at[axis] + step, 4)
        return tuple(at)

    def sibling(self):
        return self.device(self.at, 1 - self.core)

    def along(self, axis, step):
        return self.device(self.moved(axis, step), self.core)

    def plane(self, i):
        return (lax.rem(self.chip + i, 16) * 2 + self.core, self.at[2])

    def greet(self):
        sem = pltpu.get_barrier_semaphore()
        peers = [self.plane(i) for i in PLANE] + [self.along(2, d) for d in FAR_FIRST] + [self.sibling()]
        for peer in peers:
            pl.semaphore_signal(sem, inc=1, device_id=peer, device_id_type=MESH)
        return len(peers)


def remote(src, dst, send, recv, to):
    return pltpu.make_async_remote_copy(src_ref=src, dst_ref=dst, send_sem=send, recv_sem=recv, device_id=to, device_id_type=MESH)


class Part:
    def __init__(self, net, G, where, sems):
        self.net, self.G, self.where, self.sems = net, G, where, sems

    def view(self, p, phase, at, half=None):
        at = list(at)
        for axis in ORDERS[p][:phase]:
            at[axis] = slice(None)
        if half is not None:
            at[ORDERS[p][0]] = pl.ds(2 * half, 2)
        return self.G.at[(*self.where, at[2], at[1], at[0], p)]

    def start(self, phase, send, recv, ds=NEAR_FIRST):
        for d in ds:
            for p in range(3):
                ref = self.view(p, phase, self.net.at)
                remote(ref, ref, self.sems.at[send], self.sems.at[recv], self.net.along(ORDERS[p][phase], d)).start()

    def pass_along(self, send, recv):
        for p in range(3):
            for d in (1, 3):
                axis = ORDERS[p][2]
                ref = self.view(p, 2, self.net.moved(axis, 4 - d), d // 2)
                remote(ref, ref, self.sems.at[send], self.sems.at[recv], self.net.along(axis, d)).start()

    def bulk(self, blocks):
        all_ = slice(None)
        piece = {9: (0, 0, pl.ds(0, 3)), 36: (0, all_, pl.ds(0, 3)), 48: (0,), 96: (pl.ds(0, 2),), 144: (all_, all_, pl.ds(0, 3)), 192: ()}[blocks]
        return self.G.at[(*self.where, *piece)]

    def wait(self, blocks, sem):
        ref = self.bulk(blocks)
        remote(ref, ref, self.sems.at[sem], self.sems.at[sem], self.net.sibling()).wait_recv()

    def wait_sent(self, blocks, sem):
        ref = self.bulk(blocks)
        remote(ref, ref, self.sems.at[sem], self.sems.at[sem], self.net.sibling()).wait_send()

    def slab(self, p, d, send, recv):
        ref = self.view(p, 2, self.net.moved(ORDERS[p][2], 4 - d) if d else self.net.at)
        return remote(ref, ref, self.sems.at[send], self.sems.at[recv], self.net.sibling())

    def whole(self, send, recv):
        ref = self.bulk(192)
        return remote(ref, ref, self.sems.at[send], self.sems.at[recv], self.net.sibling())


def compute(rows, lens_h, tok_h, table_h, trows_h, g1_h, b1_h, ob_h, g2_h, b2_h, db_h, cot_h, qvb_h, upb_h, wq_h, wo_h, wu_h, wd_h,
            out_h, tgrad_h, pgrad_h,
            lens, tok, table, trows, g1_, b1_, ob_, g2_, b2_, db_, cot, qvb, upb, wq, wo, wu, wd,
            inp, fin, qkv, probs, dscores, att, mid, sin, hid, dup, dmid, dml, dat, dqkv, out, tgrad,
            GA, GB, GC, stage, other, bias, part, half, slots, zslots, final, pbuf, isem, psem, gsem, tsem, osem):
    images = rows // SEQ
    net = Net()
    t = net.at[2]
    n_peers = net.greet()

    loads = []
    for k, (src, dst) in enumerate(((wq_h, wq), (wo_h, wo), (wu_h, wu), (wd_h, wd), (lens_h, lens), (trows_h, trows), (table_h, table),
                                    (tok_h, tok), (qvb_h, qvb), (upb_h, upb), (g1_h, g1_), (b1_h, b1_), (ob_h, ob_), (g2_h, g2_),
                                    (b2_h, b2_), (db_h, db_), (cot_h, cot))):
        loads.append(pltpu.make_async_copy(src, dst, isem.at[k]))
    for load in loads:
        load.start()
    for load in loads[:4]:
        load.wait()
    stage[0] = jnp.concatenate([wq[0], wq[1], wq[2], wo[...]], axis=1)
    stage[1] = wu[...]
    stage[2] = wd[...]
    for load in loads[4:12]:
        load.wait()

    hots, lives = [], []
    for i in range(images):
        length = lens[t * images + i]
        base = jnp.concatenate([trows[pl.ds(t * images + i, 1), :], jnp.full((1, 384 - PROMPTS), -1, jnp.int32)], axis=1)
        slot = pltpu.roll(base, PATCHES - TAIL, 1)[:, :SEQ - TAIL]
        place = lax.broadcasted_iota(jnp.int32, (1, SEQ - TAIL), 1) + TAIL
        slot = jnp.where((place >= PATCHES) & (place < PATCHES + length), slot, -1)
        hots.append((lax.broadcasted_iota(jnp.int32, (PROMPTS, SEQ - TAIL), 0) == slot).astype(F32))
        place = lax.broadcasted_iota(jnp.int32, (SEQ - TAIL, 1), 0) + TAIL
        lives.append((place >= PATCHES) & (place < PATCHES + length))
    row = lambda ref: ref[...].reshape(1, D)
    for i in range(images):
        lo, hi = pl.ds(i * SEQ, TAIL), pl.ds(i * SEQ + TAIL, SEQ - TAIL)
        inp[lo, :] = tok[lo, :].astype(F32)
        inp[hi, :] = jnp.where(lives[i], exact(hots[i], table[...], TN), tok[hi, :].astype(F32))
        rs = pl.ds(i * SEQ, SEQ)
        fin[rs, :] = (stats(inp[rs, :])[0] * row(g1_) + row(b1_)).astype(BF)
    bias[t] = jnp.concatenate([qvb[0:1, :], jnp.zeros((1, QW), F32), qvb[1:2, :], jnp.zeros((1, 64), F32), upb[...].reshape(1, FZ)], axis=1)

    a = Part(net, GA, (net.core,), gsem)
    b = Part(net, GB, (net.core,), gsem)
    c = Part(net, GC, (slice(None), net.core, slice(None)), gsem)

    def third(j):
        return Part(net, GC, (j, net.core, slice(None)), gsem)

    pl.semaphore_wait(pltpu.get_barrier_semaphore(), n_peers)

    def pre(m):
        return remote(stage.at[m], other.at[m], psem.at[0, m], psem.at[1, m], net.sibling())

    def assemble(m, G, where, first, width):
        cs = pl.ds(pl.multiple_of(first + net.core * width, 128), width)
        mine, theirs = stage[m, :, cs], other[m, :, cs]
        own = net.core == 0
        both = jnp.concatenate([jnp.where(own, mine, theirs), jnp.where(own, theirs, mine)], axis=0).astype(BF)
        x, y, z = net.at
        for p in range(3):
            for w, lo in where:
                hi = lo + G.shape[-1]
                G[(*w, z, y, x, p)] = both[p * 16:(p + 1) * 16, lo:hi]

    def bias_copy(d):
        return remote(bias.at[t], bias.at[t], psem.at[0, 3], psem.at[1, 3], net.along(2, d))

    for m in range(3):
        pre(m).start()
    pre(0).wait_recv()
    assemble(0, GA, [((net.core,), 0)], 0, 256)
    a.start(0, 0, 1, FAR_FIRST)
    assemble(0, GB, [((net.core,), 0)], 512, 128)
    b.start(0, 2, 3, FAR_FIRST)
    for m in (1, 2):
        pre(m).wait_recv()
        assemble(m, GC, [((j, net.core, m - 1), 128 * j) for j in range(3)], 0, 384)
    c.start(0, 4, 5, FAR_FIRST)
    for d in (1, 2, 3):
        bias_copy(d).start()
    a.wait(9, 1)
    a.start(1, 6, 7, FAR_FIRST)
    b.wait(9, 3)
    b.start(1, 8, 9, FAR_FIRST)
    c.wait(9, 5)
    c.start(1, 10, 11, FAR_FIRST)
    a.wait(36, 7)
    for d, r in zip(NEAR_FIRST, (13, 14, 15)):
        a.start(2, 12, r, (d,))
    for p in range(3):
        a.slab(p, 0, 16, 17).start()
    b.wait(36, 9)
    b.start(2, 18, 19)
    c.wait(36, 11)
    for j in range(3):
        third(j).start(2, 22 + 6 * j, 23 + 6 * j, (1, 3))
    for d, r in zip(NEAR_FIRST, (13, 14, 15)):
        a.wait(48, r)
        for p in range(3):
            a.slab(p, d, 16, 17).start()
    a.wait(192, 17)
    remote(bias.at[pl.ds(0, 3)], bias.at[pl.ds(0, 3)], psem.at[0, 3], psem.at[1, 3], net.sibling()).wait()

    def w_a(z):
        return jnp.concatenate([GA[core, z].reshape(D, 256) for core in range(2)], axis=1)

    def w_b(z):
        return jnp.concatenate([GB[core, z].reshape(D, 128) for core in range(2)], axis=1)

    def pair(m, z, j):
        return jnp.concatenate([GC[j, core, m, z].reshape(D, 128) for core in range(2)], axis=1)

    x = fin[...]
    for z in range(NZ):
        qkv[z, :, 0:512] = (mm(x, w_a(z)) + bias[z, :, 0:512]).astype(BF)
    b.wait(144, 19)
    b.whole(20, 21).start()
    b.wait(192, 21)
    last = mm(fin[...], jnp.concatenate([w_b(z)[:, :HD] for z in range(NZ)], axis=1))
    for z in range(NZ):
        qkv[z, :, 512:576] = (last[:, z * 64:(z + 1) * 64] + bias[z, :, 512:576]).astype(BF)

    def attend(z):
        for i in range(images):
            rs = pl.ds(i * SEQ, SEQ)
            blk = qkv[z, rs, :]
            alive = lax.broadcasted_iota(jnp.int32, (SEQ - TAIL, 1), 0) + TAIL < PATCHES + lens[t * images + i]
            outs = []
            for h in range(HZ):
                q = (blk[:, h * HD:(h + 1) * HD] * 0.125).astype(BF)
                k = blk[:, QW + h * HD:QW + (h + 1) * HD]
                v = blk[:, 2 * QW + h * HD:2 * QW + (h + 1) * HD]
                s = mm(k, q, NT)
                s = jnp.concatenate([s[:TAIL], jnp.where(alive, s[TAIL:], MASKED)], axis=0)
                e = jnp.exp(s - jnp.max(s, axis=0, keepdims=True))
                p = (e * (1.0 / jnp.sum(e, axis=0, keepdims=True))).astype(BF)
                probs[z, i * HZ + h] = p
                outs.append(mm(p, v, TN).astype(BF))
            att[z, rs, :] = jnp.concatenate(outs, axis=1)

    def onward(j):
        third(j).wait(96, 23 + 6 * j)
        third(j).pass_along(24 + 6 * j, 25 + 6 * j)

    def relay(j):
        third(j).wait(48, 25 + 6 * j)
        third(j).whole(26 + 6 * j, 27 + 6 * j).start()

    onward(0)
    attend(0)
    attend(1)
    onward(1)
    attend(2)
    attend(3)
    onward(2)
    relay(0)

    for load_ in loads[12:]:
        load_.wait()
    wout = jnp.concatenate([w_b(z)[:, HD:] for z in range(NZ)], axis=1)
    for i in range(images):
        rs = pl.ds(i * SEQ, SEQ)
        h = inp[rs, :] + mm(jnp.concatenate([att[z, rs, :] for z in range(NZ)], axis=1), wout, NT) + row(ob_)
        mid[rs, :] = h
        sin[rs, :] = (stats(h)[0] * row(g2_) + row(b2_)).astype(BF)

    relay(1)

    @pl.loop(0, 3)
    def _(j):
        third(j).wait(192, 27 + 6 * j)
        for z in range(NZ):
            ub = jnp.concatenate([bias[z, :, pl.ds(pl.multiple_of(o + j * 128, 128), 128)] for o in (640, 1024)], axis=1)
            u = mm(sin[...], pair(0, z, j)) + ub
            dh = mm(cot[...], pair(1, z, j))
            g, slope = gelu_pair(u)
            here = pl.ds(pl.multiple_of((j * NZ + z) * 256, 256), 256)
            hid[:, here] = g.astype(BF)
            dup[:, here] = (dh * slope).astype(BF)

        @pl.when(j == 0)
        def _():
            relay(2)

    total = None
    for j in range(3):
        w = jnp.concatenate([pair(0, z, j) for z in range(NZ)], axis=1)
        piece = mm(dup[:, j * 1024:(j + 1) * 1024], w, NT)
        total = piece if total is None else total + piece
    dmid[...] = total
    for i in range(images):
        rs = pl.ds(i * SEQ, SEQ)
        n, r = stats(mid[rs, :])
        d = cot[rs, :].astype(F32) + norm_back(dmid[rs, :], n, r, row(g2_))
        dmid[rs, :] = d
        dml[rs, :] = d.astype(BF)
    wout = jnp.concatenate([w_b(z)[:, HD:] for z in range(NZ)], axis=1)
    d = mm(dml[...], wout).astype(BF)
    for z in range(NZ):
        dat[z] = d[:, z * QW:(z + 1) * QW]

    def attend_back(z):
        for i in range(images):
            rs, hi = pl.ds(i * SEQ, SEQ), pl.ds(i * SEQ + TAIL, SEQ - TAIL)
            blk = qkv[z, rs, :]
            dab = dat[z, rs, :]
            kt = blk[:, QW:2 * QW].T
            dq, dk, dv = [], [], []
            for h in range(HZ):
                v = blk[:, 2 * QW + h * HD:2 * QW + (h + 1) * HD]
                do = dab[:, h * HD:(h + 1) * HD]
                p = probs[z, i * HZ + h]
                dv.append(mm(p[TAIL:], do).astype(BF))
                pf = p.astype(F32)
                x = mm(v, do, NT) * pf
                ds = (x - pf * jnp.sum(x, axis=0, keepdims=True)).astype(BF)
                dscores[z, i * HZ + h] = ds
                dk.append((mm(ds[TAIL:], blk[:, h * HD:(h + 1) * HD]) * 0.125).astype(BF))
                dq.append(mm(kt[h * HD:(h + 1) * HD], ds[:, 128:]))
            dq = (jnp.concatenate(dq, axis=0).T[TAIL - 128:] * 0.125).astype(BF)
            dqkv[z, hi, :] = jnp.concatenate([dq] + dk + dv, axis=1)

    def attend_back_rest(z):
        for i in range(images):
            rs, lo = pl.ds(i * SEQ, SEQ), pl.ds(i * SEQ, TAIL)
            blk = qkv[z, rs, :]
            dab = dat[z, rs, :]
            kt = blk[:, QW:2 * QW].T
            dq, dk, dv = [], [], []
            for h in range(HZ):
                dv.append(mm(probs[z, i * HZ + h, :TAIL, :], dab[:, h * HD:(h + 1) * HD]).astype(BF))
                ds = dscores[z, i * HZ + h]
                dk.append((mm(ds[:TAIL], blk[:, h * HD:(h + 1) * HD]) * 0.125).astype(BF))
                dq.append(mm(kt[h * HD:(h + 1) * HD], ds[:, :256]))
            dq = (jnp.concatenate(dq, axis=0).T[:TAIL] * 0.125).astype(BF)
            dqkv[z, lo, :] = jnp.concatenate([dq] + dk + dv, axis=1)

    @pl.loop(0, NZ // 2)
    def _(w):
        attend_back(2 * w)
        attend_back(2 * w + 1)

    def d_first(slices):
        w = jnp.concatenate([w for z in range(NZ) for w in (w_a(z), w_b(z)[:, :HD])], axis=1)
        x = jnp.concatenate([jnp.concatenate([dqkv[z, sl, :] for z in range(NZ)], axis=1) for sl in slices], axis=0)
        return mm(x, w, NT)

    tails = [pl.ds(i * SEQ + TAIL, SEQ - TAIL) for i in range(images)]
    n, r = stats(jnp.concatenate([inp[sl, :] for sl in tails], axis=0))
    d = jnp.concatenate([dmid[sl, :] for sl in tails], axis=0) + norm_back(d_first(tails), n, r, row(g1_))
    total = exact(jnp.concatenate(hots, axis=1), d)
    for i, sl in enumerate(tails):
        tgrad[sl, :] = jnp.where(lives[i], 0.0, d[i * (SEQ - TAIL):(i + 1) * (SEQ - TAIL)])
    part[...] = jnp.concatenate([total, jnp.zeros((128 - PROMPTS, D), F32)], axis=0)

    core, chip = net.core, net.chip
    mine = pl.ds(pl.multiple_of(core * 384, 128), 384)
    theirs = pl.ds(pl.multiple_of((1 - core) * 384, 128), 384)
    here = pl.ds(pl.multiple_of(chip * 8, 8), 8)

    def rest(i):
        lo = pl.ds(i * SEQ, TAIL)
        n, r = stats(inp[lo, :])
        tgrad[lo, :] = dmid[lo, :] + norm_back(d_first([lo]), n, r, row(g1_))

    def down():
        @pl.loop(0, images)
        def _(i):
            rs = pl.ds(pl.multiple_of(i * SEQ, 16), SEQ)
            acc = None
            for j in range(3):
                w = jnp.concatenate([pair(1, z, j) for z in range(NZ)], axis=1)
                piece = mm(hid[rs, j * 1024:(j + 1) * 1024], w, NT)
                acc = piece if acc is None else acc + piece
            out[rs, :] = (mid[rs, :] + acc + row(db_)).astype(BF)

    swap = remote(part.at[:, theirs], half, tsem.at[0], tsem.at[1], net.sibling())
    swap.start()
    swap.wait()
    part[:, mine] = part[:, mine] + half[...]
    for i in PLANE:
        dst = lax.rem(chip + i, 16)
        remote(part.at[pl.ds(pl.multiple_of(dst * 8, 8), 8), mine], slots.at[i], tsem.at[2], tsem.at[3], net.plane(i)).start()

    @pl.loop(0, NZ // 2)
    def _(w):
        attend_back_rest(2 * w)
        attend_back_rest(2 * w + 1)

    fifteen = slots.at[pl.ds(1, 15)]
    remote(fifteen, fifteen, tsem.at[2], tsem.at[3], net.sibling()).wait()
    acc = part[here, mine]
    for i in range(1, 16):
        acc = acc + slots[i]
    zslots[t] = acc
    for d in FAR_FIRST:
        remote(zslots.at[t], zslots.at[t], tsem.at[4], tsem.at[5], net.along(2, d)).start()
    rest(0)
    rest(1)
    tout = pltpu.make_async_copy(tgrad, tgrad_h, osem.at[0])
    tout.start()
    three = zslots.at[pl.ds(0, 3)]
    remote(three, three, tsem.at[4], tsem.at[5], net.sibling()).wait()
    final[here, mine] = (zslots[0] + zslots[1]) + (zslots[2] + zslots[3])
    ref = final.at[here, mine]
    for i in PLANE:
        remote(ref, ref, tsem.at[6], tsem.at[7], net.plane(i)).start()
    down()
    oout = pltpu.make_async_copy(out, out_h, osem.at[1])
    oout.start()
    for m in range(3):
        pre(m).wait_send()
    for part_, sems in ((a, (0, 6, 12, 16)), (b, (2, 8, 18, 20))):
        for blocks, sem in zip((9, 36, 144, 192), sems):
            part_.wait_sent(blocks, sem)
    c.wait_sent(9, 4)
    c.wait_sent(36, 10)
    for j in range(3):
        third(j).wait_sent(96, 22 + 6 * j)
        third(j).wait_sent(48, 24 + 6 * j)
        third(j).wait_sent(192, 26 + 6 * j)
    many = final.at[pl.ds(0, 120), mine]
    remote(many, many, tsem.at[6], tsem.at[7], net.sibling()).wait()
    done = remote(final.at[pl.ds(0, 104), mine], final.at[pl.ds(0, 104), mine], tsem.at[8], tsem.at[9], net.sibling())
    done.start()
    done.wait()
    pbuf[...] = final[0:PROMPTS, :]
    pout = pltpu.make_async_copy(pbuf, pgrad_h, osem.at[2])
    pout.start()
    pout.wait()
    tout.wait()
    oout.wait()


def hand_over(pairs, *refs):
    n = len(pairs)
    srcs, dsts, bufs, sem = refs[:n], refs[n:2 * n], refs[2 * n:3 * n], refs[3 * n]
    pieces = []
    for src, dst, buf, rows in zip(srcs, dsts, bufs, pairs):
        for first in range(0, src.shape[0], rows):
            pieces.append((src, dst, buf, pl.ds(first, min(rows, src.shape[0] - first))))
    into = [pltpu.make_async_copy(s.at[r], b.at[r], sem.at[0, k]) for k, (s, d, b, r) in enumerate(pieces)]
    away = [pltpu.make_async_copy(b.at[r], d.at[r], sem.at[1, k]) for k, (s, d, b, r) in enumerate(pieces)]
    for copy in into:
        copy.start()
    for first, second in zip(into, away):
        first.wait()
        second.start()
    for copy in away:
        copy.wait()


def body(tokens, prompt_table, lengths, table_rows, ln1_gain, ln1_bias, w_qkv, qv_bias, w_out, out_bias,
         ln2_gain, ln2_bias, w_up, up_bias, w_down, down_bias, cotangent):
    rows = tokens.shape[0]
    images = rows // SEQ
    any_ = pl.BlockSpec(memory_space=pl.ANY)
    args = (lengths, tokens, prompt_table, table_rows, ln1_gain, ln1_bias, out_bias, ln2_gain, ln2_bias, down_bias, cotangent,
            qv_bias, up_bias, w_qkv, w_out.T, w_up, w_down.T)
    vmem = lambda shape, dtype: pltpu.VMEM(shape, dtype)
    token_out, grad_out, table_out = pl.pallas_call(
        functools.partial(compute, rows),
        out_shape=(jax.ShapeDtypeStruct((rows, D), BF), jax.ShapeDtypeStruct((rows, D), F32), jax.ShapeDtypeStruct((PROMPTS, D), F32)),
        in_specs=[any_] * len(args),
        out_specs=(any_, any_, any_),
        scratch_shapes=[pltpu.SMEM(lengths.shape, lengths.dtype)] + [vmem(v.shape, v.dtype) for v in args[1:]] + [
            vmem((rows, D), F32),
            vmem((rows, D), BF),
            vmem((NZ, rows, 3 * QW), BF),
            vmem((NZ, images * HZ, SEQ, SEQ), BF),
            vmem((NZ, images * HZ, SEQ, SEQ), BF),
            vmem((NZ, rows, QW), BF),
            vmem((rows, D), F32),
            vmem((rows, D), BF),
            vmem((rows, NZ * FZ), BF),
            vmem((rows, NZ * FZ), BF),
            vmem((rows, D), F32),
            vmem((rows, D), BF),
            vmem((NZ, rows, QW), BF),
            vmem((NZ, rows, 3 * QW), BF),
            vmem((rows, D), BF),
            vmem((rows, D), F32),
            vmem((2, 4, 4, 4, 3, 16, 256), BF),
            vmem((2, 4, 4, 4, 3, 16, 128), BF),
            vmem((3, 2, 2, 4, 4, 4, 3, 16, 128), BF),
            vmem((3, 24, 768), F32),
            vmem((3, 24, 768), F32),
            vmem((NZ, 1, 1408), F32),
            vmem((128, D), F32),
            vmem((128, 384), F32),
            vmem((16, 8, 384), F32),
            vmem((NZ, 8, 384), F32),
            vmem((128, D), F32),
            vmem((PROMPTS, D), F32),
            DMA((len(args),)), DMA((2, 4)), DMA((40,)), DMA((10,)), DMA((3,)),
        ],
        compiler_params=pltpu.CompilerParams(collective_id=1, has_side_effects=True, vmem_limit_bytes=63 * 2**20),
    )(*args)
    outs = (token_out, grad_out, table_out)
    return pl.pallas_call(
        functools.partial(hand_over, (160, 160, PROMPTS)),
        out_shape=tuple(jax.ShapeDtypeStruct(v.shape, v.dtype) for v in outs),
        in_specs=[any_] * 3,
        out_specs=(any_, any_, any_),
        scratch_shapes=[vmem(v.shape, v.dtype) for v in outs] + [DMA((2, 9))],
    )(*outs)


def solution(mesh):
    row = P(("dp", "tensor"), None)
    return jax.shard_map(
        body, mesh=mesh,
        in_specs=(row, P(), P("dp"), P("dp", None), P(), P(), P(None, "dp", "tensor"), P(None, "tensor"), P("tensor", "dp"),
                  P(), P(), P(), P("dp", "tensor"), P("tensor"), P("tensor", "dp"), P(), row),
        out_specs=(row, row, P()), check_vma=False)
```
